32 devices in a mesh: parts: 2 (over y), space: 4 (over z), dp: 2 (over x), chan: 2 (over core).
Axes of the slice: x: 2, y: 2, z: 4, core: 2. Of those that a mesh axis runs over, the one named last changes fastest.
Arguments:
- grad_out: bfloat16 [4, 4, 16, 16, 1024], P(('parts', 'dp'), 'space', None, None, 'chan'), parts along dimension 0, may hold values from -6 to 6
- saved_spectrum: bfloat16 [2, 4, 4, 16, 16, 1024], P(None, ('parts', 'dp'), None, 'space', None, 'chan'), parts along dimension 1, may hold values from -6 to 6
- w_first: bfloat16 [8, 2, 128, 128], P('chan'), may hold values from -0.375 to 0.375
- bias_first: bfloat16 [2, 1024], P(None, 'chan'), may hold values from -3 to 3
- w_second: bfloat16 [8, 2, 128, 128], P('chan'), may hold values from -0.375 to 0.375
Outputs:
- grad_in: bfloat16 [4, 4, 16, 16, 1024], P(('parts', 'dp'), 'space', None, None, 'chan'), parts along dimension 0
- grad_first: float32 [16, 2, 128, 128], P(('parts', 'chan'), None, ('space', 'dp')), parts along dimension 0
- grad_second: float32 [16, 2, 128, 128], P(('parts', 'chan'), None, ('space', 'dp')), parts along dimension 0
The draws below stay inside these ranges and needn't reach their ends.
There are 2 independent parts, one for each index of `parts`. The reference program is written for one: setup_inputs(seed, part) draws one part's arguments, and reference() takes and returns one part's arrays. A program takes and returns all parts, laid end to end along the dimension named above; an argument that names none is the same for every part. Nothing has to cross between parts.
All inputs are finite; a program needn't handle non-finite values.
Results may differ from the reference program's by a relative error of at most 0.013.
Values may be sent and summed in bfloat16 or wider, within the bound.
No kernel may reach another device: no remote copies, remote signals or barrier semaphores. Data moves between devices by JAX's collectives and lax.ppermute only.
A program may use at most 64 MiB of HBM per device.

```python
import math
import jax
import jax.numpy as jnp
from jax import lax

WIDTH = 1024
BLOCK = 128
NBLOCK = 8
GY = 16
GZ = 16
GX = 4
SAMPLES = 2


def block_levels(key, extent, pieces, smallest, high):
    factor_of = 1.0
    for axis_at, parts in pieces:
        draws = jax.random.uniform(jax.random.fold_in(jax.random.fold_in(key, 6), axis_at), (parts,), jnp.float32, smallest / len(pieces), high / len(pieces))
        factor_of = factor_of * jnp.repeat(jnp.exp(draws), extent[axis_at] // parts).reshape((-1,) + (1,) * (len(extent) - 1 - axis_at))
    return factor_of


def gaussian(rng, dims, scale, reach, pieces=(), kind=jnp.bfloat16):
    entries = scale * jax.random.normal(rng, dims, jnp.float32)
    if pieces:
        entries = entries * block_levels(rng, dims, pieces, -0.22, 0.18)
    return jnp.clip(entries, -reach, reach).astype(kind)


def setup_inputs(seed: int = 0, part: int = 0) -> dict:
    arg_keys = jax.random.split(jax.random.key(seed), 6)
    part_keys = jax.random.split(jax.random.fold_in(arg_keys[5], part), 6)
    grad_out = gaussian(part_keys[0], (SAMPLES, GX, GY, GZ, WIDTH), 1.0, 6.0, ((0, 2), (1, 4), (4, 2)))
    saved_spectrum = gaussian(part_keys[1], (2, SAMPLES, GX, GY, GZ, WIDTH), 0.8, 6.0, ((1, 2), (3, 4), (5, 2)))
    w_first = gaussian(arg_keys[2], (NBLOCK, 2, BLOCK, BLOCK), (2 * BLOCK) ** -0.5, 0.375, ((0, 2),))
    bias_first = gaussian(arg_keys[3], (2, WIDTH), 0.5, 3.0, ((1, 2),))
    w_second = gaussian(arg_keys[4], (NBLOCK, 2, BLOCK, BLOCK), (2 * BLOCK) ** -0.5, 0.375, ((0, 2),))
    return dict(grad_out=grad_out, saved_spectrum=saved_spectrum, w_first=w_first, bias_first=bias_first, w_second=w_second)


inv_root_two = 1.0 / math.sqrt(2.0)
inv_root_tau = 1.0 / math.sqrt(2.0 * math.pi)

def gelu_value(values):
    return values * 0.5 * (1.0 + lax.erf(values * inv_root_two))

def gelu_slope(values):
    return 0.5 * (1.0 + lax.erf(values * inv_root_two)) + values * jnp.exp(-0.5 * values * values) * inv_root_tau

def rounded(values):
    return lax.optimization_barrier(values.astype(jnp.bfloat16)).astype(jnp.float32)

def forward_product(left, right):
    return jnp.einsum('xyzbc,bcd->xyzbd', left, right, precision=lax.Precision.HIGHEST)

def adjoint_product(left, right):
    return jnp.einsum('xyzbd,bcd->xyzbc', left, right, precision=lax.Precision.HIGHEST)

def weight_product(left, right):
    return jnp.einsum('xyzbc,xyzbd->bcd', left, right, precision=lax.Precision.HIGHEST)

def reference(grad_out, saved_spectrum, w_first, bias_first, w_second):
    samples, length_x, length_y, length_z, width = grad_out.shape
    count = w_first.shape[0]
    block = w_first.shape[2]
    cells = length_x * length_y * length_z
    norm_scale = 1.0 / math.sqrt(cells)
    grad_scale = 1.0 / math.sqrt(cells * samples)
    first_real = w_first[:, 0].astype(jnp.float32)
    first_imag = w_first[:, 1].astype(jnp.float32)
    second_real = w_second[:, 0].astype(jnp.float32)
    second_imag = w_second[:, 1].astype(jnp.float32)
    bias = bias_first.astype(jnp.float32).reshape(2, count, block)
    blocked = (length_x, length_y, length_z, count, block)

    def one_sample(totals, inputs):
        grad, saved = inputs
        partial_spec = jnp.fft.fftn(grad.astype(jnp.float32), axes=(1, 2))
        partial_spec = lax.complex(rounded(jnp.real(partial_spec)), rounded(jnp.imag(partial_spec)))
        whole = jnp.fft.fft(partial_spec, axis=0) * norm_scale
        grad_real = rounded(jnp.real(whole)).reshape(blocked)
        grad_imag = rounded(jnp.imag(whole)).reshape(blocked)
        saved_real = saved[0].astype(jnp.float32).reshape(blocked)
        saved_imag = saved[1].astype(jnp.float32).reshape(blocked)
        pre_real = forward_product(saved_real, first_real) - forward_product(saved_imag, first_imag) + bias[0]
        pre_imag = forward_product(saved_real, first_imag) + forward_product(saved_imag, first_real) + bias[1]
        act_real = rounded(gelu_value(pre_real))
        act_imag = rounded(gelu_value(pre_imag))
        back_real = adjoint_product(grad_real, second_real) + adjoint_product(grad_imag, second_imag)
        back_imag = adjoint_product(grad_imag, second_real) - adjoint_product(grad_real, second_imag)
        slope_real = rounded(back_real * gelu_slope(pre_real))
        slope_imag = rounded(back_imag * gelu_slope(pre_imag))
        input_real = adjoint_product(slope_real, first_real) + adjoint_product(slope_imag, first_imag)
        input_imag = adjoint_product(slope_imag, first_real) - adjoint_product(slope_real, first_imag)
        second_term = jnp.stack([weight_product(act_real, grad_real) + weight_product(act_imag, grad_imag), weight_product(act_real, grad_imag) - weight_product(act_imag, grad_real)], axis=1)
        first_term = jnp.stack([weight_product(saved_real, slope_real) + weight_product(saved_imag, slope_imag), weight_product(saved_real, slope_imag) - weight_product(saved_imag, slope_real)], axis=1)
        spectrum_in = lax.complex(input_real.reshape(grad.shape), input_imag.reshape(grad.shape))
        planes_back = jnp.fft.ifft(spectrum_in, axis=0) * length_x
        planes_back = lax.complex(rounded(jnp.real(planes_back)), rounded(jnp.imag(planes_back)))
        field = jnp.fft.ifftn(planes_back, axes=(1, 2)) * (length_y * length_z)
        result = (jnp.real(field) * norm_scale).astype(jnp.bfloat16)
        return ((totals[0] + first_term, totals[1] + second_term), result)
    zeros = jnp.zeros((count, 2, block, block), jnp.float32)
    totals, grad_in = lax.scan(one_sample, (zeros, zeros), (grad_out, jnp.moveaxis(saved_spectrum, 0, 1)))
    return (grad_in, totals[0] * grad_scale, totals[1] * grad_scale)
```

```python
import functools
import math

import jax
import jax.numpy as jnp
import numpy as np
from jax import lax
from jax.experimental import pallas as pl
from jax.experimental.pallas import tpu as pltpu
from jax.sharding import PartitionSpec as P

inv_root_two = 1.0 / math.sqrt(2.0)
inv_root_tau = 1.0 / math.sqrt(2.0 * math.pi)
f32 = jnp.float32
bf16 = jnp.bfloat16
vmem_bytes = 24 * 1024 * 1024


def phase_table(length_y, length_z):
    whole = math.lcm(length_y, length_z)
    y = np.arange(length_y)
    z = np.arange(length_z)
    turns = (
        (y[:, None, None, None] * y[None, None, :, None]) * (whole // length_y)
        + (z[None, :, None, None] * z[None, None, None, :]) * (whole // length_z)
    ) % whole
    cells = length_y * length_z
    return turns.reshape(cells, cells) * (2.0 * math.pi / whole)


def round_scaled(table):
    levels = np.unique(np.abs(table).round(12))
    factors = np.linspace(1.0, 2.0, 2049)[:-1]
    scaled = factors[:, None] * levels
    error = np.abs(scaled.astype(bf16).astype(np.float64) / factors[:, None] - levels).max(axis=1)
    factor = float(factors[np.argmin(error)])
    return (table * factor).astype(bf16), factor


def transform_tables(length_y, length_z, count):
    angles = phase_table(length_y, length_z)
    cells = length_y * length_z
    rows = cells // count
    both = np.stack([np.cos(angles), -np.sin(angles)]).reshape(2, count, rows, cells)
    forward, factor = round_scaled(both.transpose(1, 0, 2, 3).reshape(count, 2 * rows, cells))
    inverse = np.ascontiguousarray(forward.transpose(0, 2, 1))
    return forward, inverse, factor


def turn(real, imag, step, length, orient):
    step %= length
    if step == 0:
        return real, imag
    if 2 * step == length:
        return -real, -imag
    if 4 * step == length or 4 * step == 3 * length:
        sign = orient if 4 * step == length else -orient
        return (-imag, real) if sign > 0 else (imag, -real)
    cosine = math.cos(2.0 * math.pi * step / length)
    sine = orient * math.sin(2.0 * math.pi * step / length)
    return cosine * real - sine * imag, sine * real + cosine * imag


def short_transform(pairs, orient):
    length = len(pairs)
    if length == 1:
        return pairs
    if length % 2 == 0:
        even = short_transform(pairs[0::2], orient)
        odd = short_transform(pairs[1::2], orient)
        half = length // 2
        out = [None] * length
        for k in range(half):
            real, imag = turn(*odd[k], k, length, orient)
            out[k] = (even[k][0] + real, even[k][1] + imag)
            out[k + half] = (even[k][0] - real, even[k][1] - imag)
        return out
    out = []
    for k in range(length):
        terms = [turn(*pairs[x], k * x, length, orient) for x in range(length)]
        out.append((sum(t[0] for t in terms), sum(t[1] for t in terms)))
    return out


def paired(weight_ref, at):
    real = weight_ref[at, 0]
    imag = weight_ref[at, 1]
    return jnp.concatenate(
        [jnp.concatenate([real, imag], axis=1), jnp.concatenate([-imag, real], axis=1)], axis=0
    )


def dot_transposed(left, right):
    return lax.dot_general(left, right, (((1,), (1,)), ((), ())), preferred_element_type=f32)


def forward_kernel(count, scale, cell_ref, table_ref, *out_refs):
    me = lax.axis_index("space")
    for step, out_ref in enumerate(out_refs):
        table = table_ref[lax.rem(me + step, count)]
        for plane in range(cell_ref.shape[0]):
            product = jnp.dot(table, cell_ref[plane], preferred_element_type=f32)
            out_ref[plane] = (product * scale).astype(bf16)


def activation_kernel(saved_ref, first_ref, bias_ref, act_ref, flip_ref, slope_ref):
    count, _, block, _ = first_ref.shape
    for at in range(count):
        lanes = slice(at * block, (at + 1) * block)
        saved = jnp.concatenate([saved_ref[0, :, lanes], saved_ref[1, :, lanes]], axis=1)
        bias = jnp.concatenate([bias_ref[0:1, lanes], bias_ref[1:2, lanes]], axis=1).astype(f32)
        pre = jnp.dot(saved, paired(first_ref, at), preferred_element_type=f32) + bias
        share = 0.5 * (1.0 + lax.erf(pre * inv_root_two))
        act_ref[at] = (pre * share).astype(bf16).T
        flip_ref[at] = saved.T
        slope_ref[at] = share + pre * jnp.exp(-0.5 * pre * pre) * inv_root_tau


def filter_kernel(
    count, samples, norm_scale, grad_scale, exchange, part_refs, act_ref, flip_ref, slope_ref,
    first_ref, second_ref, back_refs, term_refs, pencil, grad, inner, returned,
):
    me = lax.axis_index("space")
    blocks, _, block, _ = first_ref.shape
    planes = part_refs[0].shape[0] // samples
    rows = part_refs[0].shape[1] // 2
    length_x = count * planes
    tile = 16 if rows % 16 == 0 else rows
    for step, part_ref in enumerate(part_refs):
        home = lax.rem(me + count - step, count)
        for sample in range(samples):
            for plane in range(planes):
                pencil[sample, home * planes + plane] = part_ref[sample * planes + plane]
    for at in range(blocks):
        lanes = slice(at * block, (at + 1) * block)
        for sample in range(samples):
            for start in range(0, rows, tile):
                pairs = [
                    (
                        pencil[sample, x, start : start + tile, lanes].astype(f32),
                        pencil[sample, x, rows + start : rows + start + tile, lanes].astype(f32),
                    )
                    for x in range(length_x)
                ]
                for x, (real, imag) in enumerate(short_transform(pairs, -1)):
                    base = (sample * length_x + x) * rows + start
                    grad[base : base + tile, :block] = (real * norm_scale).astype(bf16)
                    grad[base : base + tile, block:] = (imag * norm_scale).astype(bf16)
        value = grad[...]
        back = dot_transposed(value, paired(second_ref, at))
        slope = (back * slope_ref[at]).astype(bf16)
        inner[...] = dot_transposed(slope, paired(first_ref, at))
        for sample in range(samples):
            for start in range(0, rows, tile):
                pairs = []
                for x in range(length_x):
                    base = (sample * length_x + x) * rows + start
                    pairs.append((inner[base : base + tile, :block], inner[base : base + tile, block:]))
                for x, (real, imag) in enumerate(short_transform(pairs, 1)):
                    returned[sample, x, start : start + tile, lanes] = real.astype(bf16)
                    returned[sample, x, rows + start : rows + start + tile, lanes] = imag.astype(bf16)
        for which, left, right in ((0, flip_ref[at], slope), (1, act_ref[at], value)):
            square = jnp.dot(left, right, preferred_element_type=f32) * grad_scale
            real = square[:block, :block] + square[block:, block:]
            imag = square[:block, block:] - square[block:, :block]
            for part, term in ((0, real), (1, imag)):
                if exchange:
                    keep_ref, send_ref = term_refs
                    split = term.reshape(count, 2, block // (2 * count), block)
                    mine = lax.axis_index("dp") == 0
                    keep_ref[:, which, at, part] = jnp.where(mine, split[:, 0], split[:, 1])
                    send_ref[:, which, at, part] = jnp.where(mine, split[:, 1], split[:, 0]).astype(bf16)
                else:
                    term_refs[0][which, at, part] = term.astype(bf16)
    for step, back_ref in enumerate(back_refs):
        home = lax.rem(me + step, count)
        for sample in range(samples):
            for plane in range(planes):
                back_ref[sample * planes + plane] = returned[sample, home * planes + plane]


def inverse_kernel(count, scale, table_ref, *refs):
    me = lax.axis_index("space")
    back_refs, out_ref = refs[:-1], refs[-1]
    for plane in range(out_ref.shape[0]):
        total = None
        for step, back_ref in enumerate(back_refs):
            table = table_ref[lax.rem(me + count - step, count)]
            product = jnp.dot(table, back_ref[plane], preferred_element_type=f32)
            total = product if total is None else total + product
        out_ref[plane] = (total * scale).astype(bf16)


def pair_sum_kernel(count, keep_ref, got_ref, own_ref, *send_refs):
    me = lax.axis_index("space")
    own_ref[...] = keep_ref[me] + got_ref[me].astype(f32)
    for step, send_ref in enumerate(send_refs):
        home = lax.rem(me + step + 1, count)
        send_ref[...] = (keep_ref[home] + got_ref[home].astype(f32)).astype(bf16)


def last_sum_kernel(own_ref, *refs):
    got_refs, out_refs = refs[:-2], refs[-2:]
    for which, out_ref in enumerate(out_refs):
        total = own_ref[which]
        for got_ref in got_refs:
            total = total + got_ref[which].astype(f32)
        out_ref[...] = total


def call(kernel, outs, args, scratch=(), flops=0, transcendentals=0, name=None):
    moved = sum(a.size * a.dtype.itemsize for a in args) + sum(
        math.prod(o.shape) * o.dtype.itemsize for o in outs
    )
    return pl.pallas_call(
        kernel,
        out_shape=tuple(outs),
        in_specs=[pl.BlockSpec(memory_space=pltpu.VMEM)] * len(args),
        out_specs=tuple(pl.BlockSpec(memory_space=pltpu.VMEM) for _ in outs),
        scratch_shapes=list(scratch),
        compiler_params=pltpu.CompilerParams(vmem_limit_bytes=vmem_bytes),
        cost_estimate=pl.CostEstimate(flops=flops, bytes_accessed=moved, transcendentals=transcendentals),
        name=name,
    )(*args)


def shifted(values, step, count, axis):
    return lax.ppermute(values, axis, [(at, (at + step) % count) for at in range(count)])


def body(grad_out, saved_spectrum, w_first, bias_first, w_second):
    samples, planes, length_y, length_z, width = grad_out.shape
    blocks, _, block, _ = w_first.shape
    count = lax.axis_size("space")
    pair = lax.axis_size("dp")
    length_x = planes * count
    cells = length_y * length_z
    rows = cells // count
    lines = samples * length_x * rows
    norm_scale = 1.0 / math.sqrt(length_x * cells)
    grad_scale = 1.0 / math.sqrt(length_x * cells * samples * pair)
    piece = block // (pair * count)
    exchange = pair == 2 and piece * pair * count == block and piece % 16 == 0
    forward, inverse, factor = transform_tables(length_y, length_z, count)
    shape = jax.ShapeDtypeStruct

    slab = shape((samples * planes, 2 * rows, width), bf16)
    parts = call(
        functools.partial(forward_kernel, count, 1.0 / factor),
        [slab] * count,
        [grad_out.reshape(samples * planes, cells, width), jnp.asarray(forward)],
        flops=4 * samples * planes * cells * cells * width,
        name="forward",
    )
    parts = [parts[0]] + [shifted(parts[s], s, count, "space") for s in range(1, count)]

    act, flip, slope = call(
        activation_kernel,
        [
            shape((blocks, 2 * block, lines), bf16),
            shape((blocks, 2 * block, lines), bf16),
            shape((blocks, lines, 2 * block), f32),
        ],
        [saved_spectrum.reshape(2, lines, width), w_first, bias_first],
        flops=8 * lines * block * block * blocks,
        transcendentals=4 * lines * width,
        name="activation",
    )

    if exchange:
        terms = [shape((count, 2, blocks, 2, piece, block), kind) for kind in (f32, bf16)]
    else:
        terms = [shape((2, blocks, 2, block, block), bf16)]

    def filter_body(*refs):
        part_refs = refs[:count]
        inputs = refs[count : count + 5]
        back_refs = refs[count + 5 : 2 * count + 5]
        term_refs = refs[2 * count + 5 : 2 * count + 5 + len(terms)]
        filter_kernel(
            count, samples, norm_scale, grad_scale, exchange, part_refs, *inputs, back_refs, term_refs,
            *refs[2 * count + 5 + len(terms) :],
        )

    results = call(
        filter_body,
        [slab] * count + terms,
        [*parts, act, flip, slope, w_first, w_second],
        scratch=[
            pltpu.VMEM((samples, length_x, 2 * rows, width), bf16),
            pltpu.VMEM((lines, 2 * block), bf16),
            pltpu.VMEM((lines, 2 * block), f32),
            pltpu.VMEM((samples, length_x, 2 * rows, width), bf16),
        ],
        flops=32 * lines * block * block * blocks,
        name="filter",
    )
    backs = results[:count]
    if exchange:
        keep, send = results[count:]
        got = shifted(send, 1, pair, "dp")
        backs = [backs[0]] + [shifted(backs[s], s, count, "space") for s in range(1, count)]
        piece_shape = (2, blocks, 2, piece, block)
        sums = call(
            functools.partial(pair_sum_kernel, count),
            [shape(piece_shape, f32)] + [shape(piece_shape, bf16)] * (count - 1),
            [keep, got],
            name="pair_sum",
        )
        others = [shifted(sums[s], s, count, "space") for s in range(1, count)]
        grad_first, grad_second = call(
            last_sum_kernel, [shape(piece_shape[1:], f32)] * 2, [sums[0], *others], name="last_sum"
        )
    else:
        backs = [backs[0]] + [shifted(backs[s], s, count, "space") for s in range(1, count)]
        term = lax.psum_scatter(results[count], "space", scatter_dimension=3, tiled=True)
        term = lax.psum_scatter(term, "dp", scatter_dimension=3, tiled=True).astype(f32)
        grad_first, grad_second = term[0], term[1]
    (grad_in,) = call(
        functools.partial(inverse_kernel, count, norm_scale / factor),
        [shape((samples * planes, cells, width), bf16)],
        [jnp.asarray(inverse), *backs],
        flops=4 * samples * planes * cells * cells * width,
        name="inverse",
    )
    return grad_in.reshape(grad_out.shape), grad_first, grad_second


def solution(mesh):
    in_specs = (
        P(("parts", "dp"), "space", None, None, "chan"),
        P(None, ("parts", "dp"), None, "space", None, "chan"),
        P("chan", None, None, None),
        P(None, "chan"),
        P("chan", None, None, None),
    )
    out_specs = (
        P(("parts", "dp"), "space", None, None, "chan"),
        P(("parts", "chan"), None, ("space", "dp"), None),
        P(("parts", "chan"), None, ("space", "dp"), None),
    )
    return jax.shard_map(body, mesh=mesh, in_specs=in_specs, out_specs=out_specs, check_vma=False)
```

```python
import functools
import math

import jax
import jax.numpy as jnp
import numpy as np
from jax import lax
from jax.experimental import pallas as pl
from jax.experimental.pallas import tpu as pltpu
from jax.sharding import PartitionSpec as P

inv_root_two = 1.0 / math.sqrt(2.0)
inv_root_tau = 1.0 / math.sqrt(2.0 * math.pi)
f32 = jnp.float32
bf16 = jnp.bfloat16
vmem_bytes = 24 * 1024 * 1024


def phase_table(length_y, length_z):
    whole = math.lcm(length_y, length_z)
    y = np.arange(length_y)
    z = np.arange(length_z)
    turns = (
        (y[:, None, None, None] * y[None, None, :, None]) * (whole // length_y)
        + (z[None, :, None, None] * z[None, None, None, :]) * (whole // length_z)
    ) % whole
    cells = length_y * length_z
    return turns.reshape(cells, cells) * (2.0 * math.pi / whole)


def round_scaled(table):
    levels = np.unique(np.abs(table).round(12))
    factors = np.linspace(1.0, 2.0, 2049)[:-1]
    scaled = factors[:, None] * levels
    error = np.abs(scaled.astype(bf16).astype(np.float64) / factors[:, None] - levels).max(axis=1)
    factor = float(factors[np.argmin(error)])
    return (table * factor).astype(bf16), factor


def inverse_table(length_y, length_z, count):
    angles = phase_table(length_y, length_z)
    cells = length_y * length_z
    rows = cells // count
    both = np.stack([np.cos(angles), -np.sin(angles)]).reshape(2, count, rows, cells)
    table, factor = round_scaled(both.transpose(1, 3, 0, 2).reshape(count, cells, 2 * rows))
    return table, factor


def turn(real, imag, step, length, orient):
    step %= length
    if step == 0:
        return real, imag
    if 2 * step == length:
        return -real, -imag
    if 4 * step == length or 4 * step == 3 * length:
        sign = orient if 4 * step == length else -orient
        return (-imag, real) if sign > 0 else (imag, -real)
    cosine = math.cos(2.0 * math.pi * step / length)
    sine = orient * math.sin(2.0 * math.pi * step / length)
    return cosine * real - sine * imag, sine * real + cosine * imag


def short_transform(pairs, orient):
    length = len(pairs)
    if length == 1:
        return pairs
    if length % 2 == 0:
        even = short_transform(pairs[0::2], orient)
        odd = short_transform(pairs[1::2], orient)
        half = length // 2
        out = [None] * length
        for k in range(half):
            real, imag = turn(*odd[k], k, length, orient)
            out[k] = (even[k][0] + real, even[k][1] + imag)
            out[k + half] = (even[k][0] - real, even[k][1] - imag)
        return out
    out = []
    for k in range(length):
        terms = [turn(*pairs[x], k * x, length, orient) for x in range(length)]
        out.append((sum(t[0] for t in terms), sum(t[1] for t in terms)))
    return out


def paired(weight_ref, at):
    real = weight_ref[at, 0]
    imag = weight_ref[at, 1]
    return jnp.concatenate(
        [jnp.concatenate([real, imag], axis=1), jnp.concatenate([-imag, real], axis=1)], axis=0
    )


def dot_transposed(left, right):
    return lax.dot_general(left, right, (((1,), (1,)), ((), ())), preferred_element_type=f32)


def wave_rows(length, cells, inner, outer):
    row = lax.broadcasted_iota(jnp.int32, (length, cells), 0)
    cell = lax.broadcasted_iota(jnp.int32, (length, cells), 1)
    angle = lax.rem(row * lax.rem(cell // inner, outer), length).astype(f32) * (2.0 * math.pi / length)
    return jnp.cos(angle), jnp.sin(angle)


def forward_kernel(count, factor, length_y, length_z, spans, cell_ref, *refs):
    out_refs, (table_ref,) = refs[:-1], refs[-1:]
    me = lax.axis_index("space")
    planes, cells, _ = cell_ref.shape
    rows = cells // count
    cos_y, sin_y = wave_rows(length_y, cells, length_z, length_y)
    cos_z, sin_z = wave_rows(length_z, cells, 1, length_z)
    cos_z, sin_z = cos_z * factor, sin_z * factor
    each = length_y // count
    for ky in range(length_y):
        cos_k, sin_k = cos_y[ky : ky + 1], sin_y[ky : ky + 1]
        start = ky % each * length_z
        table_ref[ky // each, start : start + length_z] = (cos_z * cos_k - sin_z * sin_k).astype(bf16)
        table_ref[ky // each, rows + start : rows + start + length_z] = (
            -(cos_z * sin_k) - sin_z * cos_k
        ).astype(bf16)
    for step in range(count):
        table = table_ref[lax.rem(me + step, count)]
        for plane in range(planes):
            product = jnp.dot(table, cell_ref[plane], preferred_element_type=f32) * (1.0 / factor)
            for chunk, (low, high) in enumerate(spans):
                out_refs[chunk * count + step][plane] = product[:, low:high].astype(bf16)


def activation_kernel(spans, saved_ref, first_ref, bias_ref, *out_refs):
    count, _, block, _ = first_ref.shape
    for at in range(count):
        chunk = [low <= at * block < high for low, high in spans].index(True)
        here = at - spans[chunk][0] // block
        lanes = slice(at * block, (at + 1) * block)
        saved = jnp.concatenate([saved_ref[0, :, lanes], saved_ref[1, :, lanes]], axis=1)
        bias = jnp.concatenate([bias_ref[0:1, lanes], bias_ref[1:2, lanes]], axis=1).astype(f32)
        pre = jnp.dot(saved, paired(first_ref, at), preferred_element_type=f32) + bias
        share = 0.5 * (1.0 + lax.erf(pre * inv_root_two))
        act_ref, flip_ref, slope_ref = out_refs[chunk * 3 : chunk * 3 + 3]
        act_ref[here] = (pre * share).astype(bf16).T
        flip_ref[here] = saved.T
        slope_ref[here] = share + pre * jnp.exp(-0.5 * pre * pre) * inv_root_tau


def filter_kernel(
    count, samples, norm_scale, first_block, part_refs, slope_ref, first_ref, second_ref, back_refs,
    value_ref, delta_ref, pencil, inner, returned,
):
    me = lax.axis_index("space")
    blocks = slope_ref.shape[0]
    block = first_ref.shape[2]
    planes = part_refs[0].shape[0] // samples
    rows = part_refs[0].shape[1] // 2
    length_x = count * planes
    tile = 16 if rows % 16 == 0 else rows
    for step, part_ref in enumerate(part_refs):
        home = lax.rem(me + count - step, count)
        for sample in range(samples):
            for plane in range(planes):
                pencil[sample, home * planes + plane] = part_ref[sample * planes + plane]
    for at in range(blocks):
        lanes = slice(at * block, (at + 1) * block)
        for sample in range(samples):
            for start in range(0, rows, tile):
                pairs = [
                    (
                        pencil[sample, x, start : start + tile, lanes].astype(f32),
                        pencil[sample, x, rows + start : rows + start + tile, lanes].astype(f32),
                    )
                    for x in range(length_x)
                ]
                for x, (real, imag) in enumerate(short_transform(pairs, -1)):
                    base = (sample * length_x + x) * rows + start
                    value_ref[at, base : base + tile, :block] = (real * norm_scale).astype(bf16)
                    value_ref[at, base : base + tile, block:] = (imag * norm_scale).astype(bf16)
        back = dot_transposed(value_ref[at], paired(second_ref, first_block + at))
        delta = (back * slope_ref[at]).astype(bf16)
        delta_ref[at] = delta
        inner[...] = dot_transposed(delta, paired(first_ref, first_block + at))
        for sample in range(samples):
            for start in range(0, rows, tile):
                pairs = []
                for x in range(length_x):
                    base = (sample * length_x + x) * rows + start
                    pairs.append((inner[base : base + tile, :block], inner[base : base + tile, block:]))
                for x, (real, imag) in enumerate(short_transform(pairs, 1)):
                    returned[sample, x, start : start + tile, lanes] = real.astype(bf16)
                    returned[sample, x, rows + start : rows + start + tile, lanes] = imag.astype(bf16)
    for step, back_ref in enumerate(back_refs):
        home = lax.rem(me + step, count)
        for sample in range(samples):
            for plane in range(planes):
                back_ref[sample * planes + plane] = returned[sample, home * planes + plane]


def weight_kernel(count, scale, exchange, chunks, *refs):
    groups = [refs[4 * c : 4 * c + 4] for c in range(chunks)]
    term_refs = refs[4 * chunks :]
    at = 0
    for act_ref, flip_ref, value_ref, delta_ref in groups:
        block = act_ref.shape[1] // 2
        for here in range(act_ref.shape[0]):
            lanes = slice(at * block, (at + 1) * block)
            for which, left, right in ((0, flip_ref, delta_ref), (1, act_ref, value_ref)):
                square = jnp.dot(left[here], right[here], preferred_element_type=f32) * scale
                real = square[:block, :block] + square[block:, block:]
                imag = square[:block, block:] - square[block:, :block]
                for part, term in ((0, real), (1, imag)):
                    if exchange:
                        keep_ref, send_refs = term_refs[0], term_refs[1:]
                        piece = block // (2 * count)
                        split = term.reshape(count, 2, piece, block)
                        mine = lax.axis_index("dp") == 0
                        place = slice((2 * which + part) * piece, (2 * which + part + 1) * piece)
                        keep_ref[:, place, lanes] = jnp.where(mine, split[:, 0], split[:, 1])
                        short = slice(part * piece, (part + 1) * piece)
                        send_refs[which][:, short, lanes] = jnp.where(mine, split[:, 1], split[:, 0]).astype(bf16)
                    else:
                        term_refs[0][which, at, part] = term.astype(bf16)
            at += 1


def inverse_kernel(count, scale, low, high, table_ref, *refs):
    me = lax.axis_index("space")
    back_refs, (out_ref, held, sem) = refs[:count], refs[-3:]
    for plane in range(held.shape[0]):
        total = None
        for step, back_ref in enumerate(back_refs):
            table = table_ref[lax.rem(me + count - step, count)]
            product = jnp.dot(table, back_ref[plane], preferred_element_type=f32)
            total = product if total is None else total + product
        held[plane] = (total * scale).astype(bf16)
    copy = pltpu.make_async_copy(held, out_ref.at[:, :, low:high], sem)
    copy.start()
    copy.wait()


def pair_sum_kernel(count, extra, keep_ref, low_ref, high_ref, *refs):
    me = lax.axis_index("space")
    for step, out_ref in enumerate(refs[extra:]):
        home = lax.rem(me + step, count)
        half = low_ref.shape[1]
        out_ref[:half] = (keep_ref[home, :half] + low_ref[home].astype(f32)).astype(out_ref.dtype)
        out_ref[half:] = (keep_ref[home, half:] + high_ref[home].astype(f32)).astype(out_ref.dtype)


def last_sum_kernel(*refs):
    got_refs, out_refs = refs[:-2], refs[-2:]
    blocks, _, piece, block = out_refs[0].shape
    total = got_refs[0][...]
    for got_ref in got_refs[1:]:
        total = total + got_ref[...].astype(f32)
    for at in range(blocks):
        for which in range(2):
            for part in range(2):
                place = (2 * which + part) * piece
                out_refs[which][at, part] = total[place : place + piece, at * block : (at + 1) * block]


def call(kernel, outs, args, scratch=(), flops=0, transcendentals=0, name=None, **extra):
    whole = pl.BlockSpec(memory_space=pltpu.VMEM)
    return pl.pallas_call(
        kernel,
        out_shape=tuple(outs),
        in_specs=extra.pop("in_specs", [whole] * len(args)),
        out_specs=extra.pop("out_specs", (whole,) * len(outs)),
        scratch_shapes=list(scratch),
        compiler_params=pltpu.CompilerParams(vmem_limit_bytes=vmem_bytes),
        cost_estimate=pl.CostEstimate(flops=0, bytes_accessed=0, transcendentals=0),
        name=name,
        **extra,
    )(*args)


def shifted(values, step, count, axis):
    return lax.ppermute(values, axis, [(at, (at + step) % count) for at in range(count)])


def body(grad_out, saved_spectrum, w_first, bias_first, w_second):
    samples, planes, length_y, length_z, width = grad_out.shape
    blocks, _, block, _ = w_first.shape
    count = lax.axis_size("space")
    pair = lax.axis_size("dp")
    length_x = planes * count
    cells = length_y * length_z
    rows = cells // count
    lines = samples * length_x * rows
    norm_scale = 1.0 / math.sqrt(length_x * cells)
    grad_scale = 1.0 / math.sqrt(length_x * cells * samples * pair)
    piece = block // (pair * count)
    exchange = pair == 2 and piece * pair * count == block and piece % 16 == 0
    sizes = (blocks,)
    chunks = len(sizes)
    spans = [(sum(sizes[:c]) * block, sum(sizes[: c + 1]) * block) for c in range(chunks)]
    slabs = samples * planes
    inverse, factor = inverse_table(length_y, length_z, count)
    shape = jax.ShapeDtypeStruct
    far_first = sorted(range(1, count), key=lambda s: -min(s, count - s))

    def spread(values):
        moved = {s: shifted(values[s], s, count, "space") for s in far_first}
        return [values[0]] + [moved[s] for s in range(1, count)]

    outs = call(
        functools.partial(forward_kernel, count, factor, length_y, length_z, spans),
        [shape((slabs, 2 * rows, high - low), bf16) for low, high in spans for _ in range(count)],
        [grad_out.reshape(slabs, cells, width)],
        scratch=[pltpu.VMEM((count, 2 * rows, cells), bf16)],
        flops=4 * slabs * cells * cells * width,
        name="forward",
    )
    parts = [spread(outs[c * count : (c + 1) * count]) for c in range(chunks)]

    active = call(
        functools.partial(activation_kernel, spans),
        [
            shape((each,) + dims, kind)
            for each in sizes
            for dims, kind in (
                ((2 * block, lines), bf16),
                ((2 * block, lines), bf16),
                ((lines, 2 * block), f32),
            )
        ],
        [saved_spectrum.reshape(2, lines, width), w_first, bias_first],
        flops=8 * lines * block * block * blocks,
        transcendentals=4 * lines * width,
        name="activation",
    )

    inverses = []
    groups = []
    for chunk, (low, high) in enumerate(spans):
        each = sizes[chunk]
        lanes = high - low
        act, flip, slope = active[3 * chunk : 3 * chunk + 3]

        def filter_body(*refs, low=low):
            filter_kernel(
                count, samples, norm_scale, low // block, refs[:count], *refs[count : count + 3],
                refs[count + 3 : 2 * count + 3], *refs[2 * count + 3 :],
            )

        results = call(
            filter_body,
            [shape((slabs, 2 * rows, lanes), bf16)] * count + [shape((each, lines, 2 * block), bf16)] * 2,
            [*parts[chunk], slope, w_first, w_second],
            scratch=[
                pltpu.VMEM((samples, length_x, 2 * rows, lanes), bf16),
                pltpu.VMEM((lines, 2 * block), f32),
                pltpu.VMEM((samples, length_x, 2 * rows, lanes), bf16),
            ],
            flops=16 * lines * block * block * each,
            name="filter" + str(chunk),
        )
        groups += [act, flip, *results[count:]]
        inverses.append(([jnp.asarray(inverse), *spread(results[:count])], low, high))

    if exchange:
        terms = [shape((count, 4 * piece, width), f32)] + [shape((count, 2 * piece, width), bf16)] * 2
    else:
        terms = [shape((2, blocks, 2, block, block), bf16)]
    terms = call(
        functools.partial(weight_kernel, count, grad_scale, exchange, chunks), terms, groups,
        flops=16 * lines * block * block * blocks, name="weight",
    )
    grad_in = None

    def invert(out, args, low, high):
        aliases = {}
        if out is not None:
            aliases = {len(args): 0}
            args = args + [out]

        return call(
            functools.partial(inverse_kernel, count, norm_scale / factor, low, high),
            [shape((slabs, cells, width), bf16)],
            args,
            in_specs=[pl.BlockSpec(memory_space=pltpu.VMEM)] * (count + 1)
            + [pl.BlockSpec(memory_space=pl.ANY)] * len(aliases),
            out_specs=(pl.BlockSpec(memory_space=pl.ANY),),
            scratch=[pltpu.VMEM((slabs, cells, high - low), bf16), pltpu.SemaphoreType.DMA],
            input_output_aliases=aliases,
            flops=4 * slabs * cells * cells * (high - low),
            name="inverse" + str(low // block),
        )[0]

    if exchange:
        keep = terms[0]
        got = [shifted(send, 1, pair, "dp") for send in terms[1:]]
        ties = [inverses[0][0][1 + far_first[0]]]
        sums = call(
            functools.partial(pair_sum_kernel, count, len(ties)),
            [shape((4 * piece, width), f32)] + [shape((4 * piece, width), bf16)] * (count - 1),
            [keep, *got, *ties],
            in_specs=[pl.BlockSpec(memory_space=pltpu.VMEM)] * 3
            + [pl.BlockSpec(memory_space=pl.ANY)] * len(ties),
            name="pair_sum",
        )
        grad_first, grad_second = call(
            last_sum_kernel,
            [shape((blocks, 2, piece, block), f32)] * 2,
            spread(sums),
            name="last_sum",
        )
    else:
        term = lax.psum_scatter(terms[0], "space", scatter_dimension=3, tiled=True)
        term = lax.psum_scatter(term, "dp", scatter_dimension=3, tiled=True).astype(f32)
        grad_first, grad_second = term[0], term[1]
    for piece_args in inverses:
        grad_in = invert(grad_in, *piece_args)
    return grad_in.reshape(grad_out.shape), grad_first, grad_second


def solution(mesh):
    in_specs = (
        P(("parts", "dp"), "space", None, None, "chan"),
        P(None, ("parts", "dp"), None, "space", None, "chan"),
        P("chan", None, None, None),
        P(None, "chan"),
        P("chan", None, None, None),
    )
    out_specs = (
        P(("parts", "dp"), "space", None, None, "chan"),
        P(("parts", "chan"), None, ("space", "dp"), None),
        P(("parts", "chan"), None, ("space", "dp"), None),
    )
    return jax.shard_map(body, mesh=mesh, in_specs=in_specs, out_specs=out_specs, check_vma=False)
```

```python
import functools
import math

import jax
import jax.numpy as jnp
import numpy as np
from jax import lax
from jax.experimental import pallas as pl
from jax.experimental.pallas import tpu as pltpu
from jax.sharding import PartitionSpec as P

inv_root_two = 1.0 / math.sqrt(2.0)
inv_root_tau = 1.0 / math.sqrt(2.0 * math.pi)
f32 = jnp.float32
bf16 = jnp.bfloat16
vmem_bytes = 24 * 1024 * 1024


def phase_table(length_y, length_z):
    whole = math.lcm(length_y, length_z)
    y = np.arange(length_y)
    z = np.arange(length_z)
    turns = (
        (y[:, None, None, None] * y[None, None, :, None]) * (whole // length_y)
        + (z[None, :, None, None] * z[None, None, None, :]) * (whole // length_z)
    ) % whole
    cells = length_y * length_z
    return turns.reshape(cells, cells) * (2.0 * math.pi / whole)


def round_scaled(table):
    levels = np.unique(np.abs(table).round(12))
    factors = np.linspace(1.0, 2.0, 2049)[:-1]
    scaled = factors[:, None] * levels
    error = np.abs(scaled.astype(bf16).astype(np.float64) / factors[:, None] - levels).max(axis=1)
    factor = float(factors[np.argmin(error)])
    return (table * factor).astype(bf16), factor


def inverse_table(length_y, length_z, count):
    angles = phase_table(length_y, length_z)
    cells = length_y * length_z
    rows = cells // count
    both = np.stack([np.cos(angles), -np.sin(angles)]).reshape(2, count, rows, cells)
    table, factor = round_scaled(both.transpose(1, 3, 0, 2).reshape(count, cells, 2 * rows))
    return table, factor


def turn(real, imag, step, length, orient):
    step %= length
    if step == 0:
        return real, imag
    if 2 * step == length:
        return -real, -imag
    if 4 * step == length or 4 * step == 3 * length:
        sign = orient if 4 * step == length else -orient
        return (-imag, real) if sign > 0 else (imag, -real)
    cosine = math.cos(2.0 * math.pi * step / length)
    sine = orient * math.sin(2.0 * math.pi * step / length)
    return cosine * real - sine * imag, sine * real + cosine * imag


def short_transform(pairs, orient):
    length = len(pairs)
    if length == 1:
        return pairs
    if length % 2 == 0:
        even = short_transform(pairs[0::2], orient)
        odd = short_transform(pairs[1::2], orient)
        half = length // 2
        out = [None] * length
        for k in range(half):
            real, imag = turn(*odd[k], k, length, orient)
            out[k] = (even[k][0] + real, even[k][1] + imag)
            out[k + half] = (even[k][0] - real, even[k][1] - imag)
        return out
    out = []
    for k in range(length):
        terms = [turn(*pairs[x], k * x, length, orient) for x in range(length)]
        out.append((sum(t[0] for t in terms), sum(t[1] for t in terms)))
    return out


def paired(weight_ref, at):
    real = weight_ref[at, 0]
    imag = weight_ref[at, 1]
    return jnp.concatenate(
        [jnp.concatenate([real, imag], axis=1), jnp.concatenate([-imag, real], axis=1)], axis=0
    )


def wave_rows(length, cells, inner, outer):
    row = lax.broadcasted_iota(jnp.int32, (length, cells), 0)
    cell = lax.broadcasted_iota(jnp.int32, (length, cells), 1)
    angle = lax.rem(row * lax.rem(cell // inner, outer), length).astype(f32) * (2.0 * math.pi / length)
    return jnp.cos(angle), jnp.sin(angle)


RING = (0, 0, 1)
EARLY = (2, 3)
AFTER = 1
TIE = 2


def ring_order(count, phase):
    if not RING[phase]:
        return list(range(count))
    return [0] + list(range(1, count, 2)) + list(range(count - 2 + count % 2, 0, -2))


def neighbour(me, step, count, phase):
    order = ring_order(count, phase)
    home = jnp.int32(0)
    for at, here in enumerate(order):
        home = jnp.where(me == here, order[(at + step) % count], home)
    return home


def forward_kernel(count, factor, length_y, length_z, cell_ref, *refs):
    out_refs, table_ref = refs[:-1], refs[-1]
    me = lax.axis_index("space")
    planes, cells, _ = cell_ref.shape
    rows = cells // count
    cos_y, sin_y = wave_rows(length_y, cells, length_z, length_y)
    cos_z, sin_z = wave_rows(length_z, cells, 1, length_z)
    cos_z, sin_z = cos_z * factor, sin_z * factor
    each = length_y // count
    for ky in range(length_y):
        cos_k, sin_k = cos_y[ky : ky + 1], sin_y[ky : ky + 1]
        start = ky % each * length_z
        table_ref[ky // each, start : start + length_z] = (cos_z * cos_k - sin_z * sin_k).astype(bf16)
        table_ref[ky // each, rows + start : rows + start + length_z] = (
            -(cos_z * sin_k) - sin_z * cos_k
        ).astype(bf16)
    for step, out_ref in enumerate(out_refs):
        table = table_ref[neighbour(me, step, count, 0)]
        for plane in range(planes):
            product = jnp.dot(table, cell_ref[plane], preferred_element_type=f32) * (1.0 / factor)
            out_ref[plane] = product.astype(bf16)


def activation_kernel(
    saved_ref, first_ref, bias_ref, second_ref, act_ref, flip_ref, slope_ref, first_back_ref, second_back_ref
):
    count, _, block, _ = first_ref.shape
    for at in range(count):
        lanes = slice(at * block, (at + 1) * block)
        first = paired(first_ref, at)
        first_back_ref[at] = first.T
        second_back_ref[at] = paired(second_ref, at).T
        saved = jnp.concatenate([saved_ref[0, :, lanes], saved_ref[1, :, lanes]], axis=1)
        bias = jnp.concatenate([bias_ref[0:1, lanes], bias_ref[1:2, lanes]], axis=1).astype(f32)
        pre = jnp.dot(saved, first, preferred_element_type=f32) + bias
        share = 0.5 * (1.0 + lax.erf(pre * inv_root_two))
        act_ref[at] = (pre * share).astype(bf16).T
        flip_ref[at] = saved.T
        slope_ref[at] = share + pre * jnp.exp(-0.5 * pre * pre) * inv_root_tau


def filter_kernel(
    count, samples, norm_scale, part_refs, slope_ref, first_back_ref, second_back_ref, back_refs,
    value_ref, delta_ref, pencil, inner, returned,
):
    me = lax.axis_index("space")
    blocks = slope_ref.shape[0]
    block = first_back_ref.shape[1] // 2
    planes = part_refs[0].shape[0] // samples
    rows = part_refs[0].shape[1] // 2
    length_x = count * planes
    tile = 16 if rows % 16 == 0 else rows
    for step, part_ref in enumerate(part_refs):
        home = neighbour(me, -step, count, 0)
        for sample in range(samples):
            for plane in range(planes):
                pencil[sample, home * planes + plane] = part_ref[sample * planes + plane]
    for at in range(blocks):
        lanes = slice(at * block, (at + 1) * block)
        for sample in range(samples):
            for start in range(0, rows, tile):
                pairs = [
                    (
                        pencil[sample, x, start : start + tile, lanes].astype(f32),
                        pencil[sample, x, rows + start : rows + start + tile, lanes].astype(f32),
                    )
                    for x in range(length_x)
                ]
                for x, (real, imag) in enumerate(short_transform(pairs, -1)):
                    base = (sample * length_x + x) * rows + start
                    value_ref[at, base : base + tile, :block] = (real * norm_scale).astype(bf16)
                    value_ref[at, base : base + tile, block:] = (imag * norm_scale).astype(bf16)
        back = jnp.dot(value_ref[at], second_back_ref[at], preferred_element_type=f32)
        delta = (back * slope_ref[at]).astype(bf16)
        delta_ref[at] = delta
        inner[at] = jnp.dot(delta, first_back_ref[at], preferred_element_type=f32)
        for sample in range(samples):
            for start in range(0, rows, tile):
                pairs = []
                for x in range(length_x):
                    base = (sample * length_x + x) * rows + start
                    pairs.append((inner[at, base : base + tile, :block], inner[at, base : base + tile, block:]))
                for x, (real, imag) in enumerate(short_transform(pairs, 1)):
                    returned[sample, x, start : start + tile, lanes] = real.astype(bf16)
                    returned[sample, x, rows + start : rows + start + tile, lanes] = imag.astype(bf16)
    for step, back_ref in enumerate(back_refs):
        home = neighbour(me, step, count, 1)
        for sample in range(samples):
            for plane in range(planes):
                back_ref[sample * planes + plane] = returned[sample, home * planes + plane]


def weight_kernel(count, scale, exchange, groups, act_ref, flip_ref, value_ref, delta_ref, *term_refs):
    block = act_ref.shape[1] // 2
    for at in range(act_ref.shape[0]):
        lanes = slice(at * block, (at + 1) * block)
        for which, left, right in ((0, flip_ref, delta_ref), (1, act_ref, value_ref)):
            square = jnp.dot(left[at], right[at], preferred_element_type=f32) * scale
            real = square[:block, :block] + square[block:, block:]
            imag = square[:block, block:] - square[block:, :block]
            for part, term in ((0, real), (1, imag)):
                if exchange:
                    keep_ref, send_ref = term_refs[0], term_refs[-1]
                    piece = block // (2 * count)
                    split = term.reshape(count, 2, piece, block)
                    mine = lax.axis_index("dp") == 0
                    place = slice((2 * which + part) * piece, (2 * which + part + 1) * piece)
                    keep_ref[:, place, lanes] = jnp.where(mine, split[:, 0], split[:, 1])
                    send_ref[:, place, lanes] = jnp.where(mine, split[:, 1], split[:, 0]).astype(bf16)
                else:
                    term_refs[0][which, at, part] = term.astype(bf16)
    if exchange:
        me = lax.axis_index("space")
        for steps, out_ref in zip(groups, term_refs[1:-1]):
            for slot, step in enumerate(steps):
                out_ref[slot] = term_refs[-1][neighbour(me, step, count, 2)]


def inverse_kernel(count, scale, table_ref, *refs):
    me = lax.axis_index("space")
    back_refs, out_ref = refs[:-1], refs[-1]
    for plane in range(out_ref.shape[0]):
        total = None
        for step, back_ref in enumerate(back_refs):
            table = table_ref[neighbour(me, -step, count, 1)]
            product = jnp.dot(table, back_ref[plane], preferred_element_type=f32)
            total = product if total is None else total + product
        out_ref[plane] = (total * scale).astype(bf16)


def pair_sum_kernel(count, steps, keep_ref, got_ref, *refs):
    me = lax.axis_index("space")
    for slot, step in enumerate(steps):
        out_ref = refs[len(refs) - len(steps) + slot]
        out_ref[...] = (keep_ref[neighbour(me, step, count, 2)] + got_ref[slot].astype(f32)).astype(out_ref.dtype)


def last_sum_kernel(*refs):
    got_refs, out_refs = refs[:-2], refs[-2:]
    blocks, _, piece, block = out_refs[0].shape
    total = got_refs[0][...]
    for got_ref in got_refs[1:]:
        total = total + got_ref[...].astype(f32)
    for at in range(blocks):
        for which in range(2):
            for part in range(2):
                place = (2 * which + part) * piece
                out_refs[which][at, part] = total[place : place + piece, at * block : (at + 1) * block]


def call(kernel, outs, args, scratch=(), loose=0, name=None):
    whole = pl.BlockSpec(memory_space=pltpu.VMEM)
    return pl.pallas_call(
        kernel,
        out_shape=tuple(outs),
        in_specs=[whole] * (len(args) - loose) + [pl.BlockSpec(memory_space=pl.ANY)] * loose,
        out_specs=(whole,) * len(outs),
        scratch_shapes=list(scratch),
        compiler_params=pltpu.CompilerParams(vmem_limit_bytes=vmem_bytes),
        name=name,
    )(*args)


def spread(values, count, phase):
    order = ring_order(count, phase)
    moved = []
    for step in range(1, count):
        pairs = [(order[at], order[(at + step) % count]) for at in range(count)]
        moved.append(lax.ppermute(values[step], "space", pairs))
    return [values[0]] + moved


def body(grad_out, saved_spectrum, w_first, bias_first, w_second):
    samples, planes, length_y, length_z, width = grad_out.shape
    blocks, _, block, _ = w_first.shape
    count = lax.axis_size("space")
    pair = lax.axis_size("dp")
    length_x = planes * count
    cells = length_y * length_z
    rows = cells // count
    lines = samples * length_x * rows
    slabs = samples * planes
    norm_scale = 1.0 / math.sqrt(length_x * cells)
    grad_scale = 1.0 / math.sqrt(length_x * cells * samples * pair)
    piece = block // (pair * count)
    exchange = pair == 2 and piece * pair * count == block and piece % 16 == 0
    inverse, factor = inverse_table(length_y, length_z, count)
    shape = jax.ShapeDtypeStruct
    slab = shape((slabs, 2 * rows, width), bf16)
    square = shape((blocks, 2 * block, 2 * block), bf16)
    tall = shape((blocks, lines, 2 * block), bf16)
    wide = shape((blocks, 2 * block, lines), bf16)

    parts = spread(
        call(
            functools.partial(forward_kernel, count, factor, length_y, length_z),
            [slab] * count,
            [grad_out.reshape(slabs, cells, width)],
            scratch=[pltpu.VMEM((count, 2 * rows, cells), bf16)],
            name="forward",
        ),
        count,
        0,
    )
    act, flip, slope, first_back, second_back = call(
        activation_kernel,
        [wide, wide, shape((blocks, lines, 2 * block), f32), square, square],
        [saved_spectrum.reshape(2, lines, width), w_first, bias_first, w_second],
        name="activation",
    )

    def filter_body(*refs):
        filter_kernel(
            count, samples, norm_scale, refs[:count], *refs[count : count + 3], refs[count + 3 : 2 * count + 3],
            *refs[2 * count + 3 :],
        )

    *backs, value, delta = call(
        filter_body,
        [slab] * count + [tall, tall],
        [*parts, slope, first_back, second_back],
        scratch=[
            pltpu.VMEM((samples, length_x, 2 * rows, width), bf16),
            pltpu.VMEM((blocks, lines, 2 * block), f32),
            pltpu.VMEM((samples, length_x, 2 * rows, width), bf16),
        ],
        name="filter",
    )
    backs = spread(backs, count, 1)
    early = EARLY if count == 4 else tuple(range(1, count // 2 + 1))
    groups = (early, (0,) + tuple(step for step in range(1, count) if step not in early))
    if exchange:
        terms = [shape((count, 4 * piece, width), f32)]
        terms += [shape((len(steps), 4 * piece, width), bf16) for steps in groups]
        scratch = [pltpu.VMEM((count, 4 * piece, width), bf16)]
    else:
        terms = [shape((2, blocks, 2, block, block), bf16)]
        scratch = []
    terms = call(
        functools.partial(weight_kernel, count, grad_scale, exchange, groups), terms, [act, flip, value, delta],
        scratch=scratch, name="weight",
    )
    if exchange:
        keep, *sends = terms
        got = [lax.ppermute(send, "dp", [(0, 1), (1, 0)]) for send in sends]
        sums = {}
        for at, steps in enumerate(groups):
            after = [backs[TIE]] if at == AFTER else []
            outs = call(
                functools.partial(pair_sum_kernel, count, steps),
                [shape((4 * piece, width), bf16 if step else f32) for step in steps],
                [keep, got[at], *after],
                loose=len(after),
                name="pair_sum" + str(at),
            )
            sums.update(zip(steps, outs))
        grad_first, grad_second = call(
            last_sum_kernel, [shape((blocks, 2, piece, block), f32)] * 2, spread([sums[step] for step in range(count)], count, 2), name="last_sum"
        )
    else:
        term = lax.psum_scatter(terms[0], "space", scatter_dimension=3, tiled=True)
        term = lax.psum_scatter(term, "dp", scatter_dimension=3, tiled=True).astype(f32)
        grad_first, grad_second = term[0], term[1]
    (grad_in,) = call(
        functools.partial(inverse_kernel, count, norm_scale / factor),
        [shape((slabs, cells, width), bf16)],
        [jnp.asarray(inverse), *backs],
        name="inverse",
    )
    return grad_in.reshape(grad_out.shape), grad_first, grad_second


def solution(mesh):
    in_specs = (
        P(("parts", "dp"), "space", None, None, "chan"),
        P(None, ("parts", "dp"), None, "space", None, "chan"),
        P("chan", None, None, None),
        P(None, "chan"),
        P("chan", None, None, None),
    )
    out_specs = (
        P(("parts", "dp"), "space", None, None, "chan"),
        P(("parts", "chan"), None, ("space", "dp"), None),
        P(("parts", "chan"), None, ("space", "dp"), None),
    )
    return jax.shard_map(body, mesh=mesh, in_specs=in_specs, out_specs=out_specs, check_vma=False)
```

```python
import functools
import math

import jax
import jax.numpy as jnp
import numpy as np
from jax import lax
from jax.experimental import pallas as pl
from jax.experimental.pallas import tpu as pltpu
from jax.sharding import PartitionSpec as P

inv_root_two = 1.0 / math.sqrt(2.0)
inv_root_tau = 1.0 / math.sqrt(2.0 * math.pi)
f32 = jnp.float32
bf16 = jnp.bfloat16
vmem_bytes = 24 * 1024 * 1024


def phase_table(length_y, length_z):
    whole = math.lcm(length_y, length_z)
    y = np.arange(length_y)
    z = np.arange(length_z)
    turns = (
        (y[:, None, None, None] * y[None, None, :, None]) * (whole // length_y)
        + (z[None, :, None, None] * z[None, None, None, :]) * (whole // length_z)
    ) % whole
    cells = length_y * length_z
    return turns.reshape(cells, cells) * (2.0 * math.pi / whole)


def round_scaled(table):
    levels = np.unique(np.abs(table).round(12))
    factors = np.linspace(1.0, 2.0, 2049)[:-1]
    scaled = factors[:, None] * levels
    error = np.abs(scaled.astype(bf16).astype(np.float64) / factors[:, None] - levels).max(axis=1)
    factor = float(factors[np.argmin(error)])
    return (table * factor).astype(bf16), factor


def inverse_table(length_y, length_z, count):
    angles = phase_table(length_y, length_z)
    cells = length_y * length_z
    rows = cells // count
    both = np.stack([np.cos(angles), -np.sin(angles)]).reshape(2, count, rows, cells)
    table, factor = round_scaled(both.transpose(1, 3, 0, 2).reshape(count, cells, 2 * rows))
    return table, factor


def turn(real, imag, step, length, orient):
    step %= length
    if step == 0:
        return real, imag
    if 2 * step == length:
        return -real, -imag
    if 4 * step == length or 4 * step == 3 * length:
        sign = orient if 4 * step == length else -orient
        return (-imag, real) if sign > 0 else (imag, -real)
    cosine = math.cos(2.0 * math.pi * step / length)
    sine = orient * math.sin(2.0 * math.pi * step / length)
    return cosine * real - sine * imag, sine * real + cosine * imag


def short_transform(pairs, orient):
    length = len(pairs)
    if length == 1:
        return pairs
    if length % 2 == 0:
        even = short_transform(pairs[0::2], orient)
        odd = short_transform(pairs[1::2], orient)
        half = length // 2
        out = [None] * length
        for k in range(half):
            real, imag = turn(*odd[k], k, length, orient)
            out[k] = (even[k][0] + real, even[k][1] + imag)
            out[k + half] = (even[k][0] - real, even[k][1] - imag)
        return out
    out = []
    for k in range(length):
        terms = [turn(*pairs[x], k * x, length, orient) for x in range(length)]
        out.append((sum(t[0] for t in terms), sum(t[1] for t in terms)))
    return out


def paired(weight_ref, at):
    real = weight_ref[at, 0]
    imag = weight_ref[at, 1]
    return jnp.concatenate(
        [jnp.concatenate([real, imag], axis=1), jnp.concatenate([-imag, real], axis=1)], axis=0
    )


def wave_rows(length, cells, inner, outer):
    row = lax.broadcasted_iota(jnp.int32, (length, cells), 0)
    cell = lax.broadcasted_iota(jnp.int32, (length, cells), 1)
    angle = lax.rem(row * lax.rem(cell // inner, outer), length).astype(f32) * (2.0 * math.pi / length)
    return jnp.cos(angle), jnp.sin(angle)


def ring(count, folded):
    if not folded:
        return list(range(count))
    return [0] + list(range(1, count, 2)) + list(range(count - 2 + count % 2, 0, -2))


def neighbour(me, step, count, folded=False):
    order = ring(count, folded)
    if not folded:
        return lax.rem(me + step + count, count)
    home = jnp.int32(0)
    for at, here in enumerate(order):
        home = jnp.where(me == here, order[(at + step) % count], home)
    return home


def forward_kernel(count, factor, length_y, length_z, cell_ref, *refs):
    out_refs, table_ref = refs[:-1], refs[-1]
    me = lax.axis_index("space")
    planes, cells, _ = cell_ref.shape
    rows = cells // count
    cos_y, sin_y = wave_rows(length_y, cells, length_z, length_y)
    cos_z, sin_z = wave_rows(length_z, cells, 1, length_z)
    cos_z, sin_z = cos_z * factor, sin_z * factor
    each = length_y // count
    for ky in range(length_y):
        cos_k, sin_k = cos_y[ky : ky + 1], sin_y[ky : ky + 1]
        start = ky % each * length_z
        table_ref[ky // each, start : start + length_z] = (cos_z * cos_k - sin_z * sin_k).astype(bf16)
        table_ref[ky // each, rows + start : rows + start + length_z] = (
            -(cos_z * sin_k) - sin_z * cos_k
        ).astype(bf16)
    for step, out_ref in enumerate(out_refs):
        table = table_ref[neighbour(me, step, count)]
        for plane in range(planes):
            product = jnp.dot(table, cell_ref[plane], preferred_element_type=f32) * (1.0 / factor)
            out_ref[plane] = product.astype(bf16)


def activation_kernel(
    saved_ref, first_ref, bias_ref, second_ref, act_ref, flip_ref, slope_ref, first_back_ref, second_back_ref
):
    count, _, block, _ = first_ref.shape
    for at in range(count):
        lanes = slice(at * block, (at + 1) * block)
        first = paired(first_ref, at)
        first_back_ref[at] = first.T
        second_back_ref[at] = paired(second_ref, at).T
        saved = jnp.concatenate([saved_ref[0, :, lanes], saved_ref[1, :, lanes]], axis=1)
        bias = jnp.concatenate([bias_ref[0:1, lanes], bias_ref[1:2, lanes]], axis=1).astype(f32)
        pre = jnp.dot(saved, first, preferred_element_type=f32) + bias
        share = 0.5 * (1.0 + lax.erf(pre * inv_root_two))
        act_ref[at] = (pre * share).astype(bf16).T
        flip_ref[at] = saved.T
        slope_ref[at] = share + pre * jnp.exp(-0.5 * pre * pre) * inv_root_tau


def filter_kernel(
    count, samples, norm_scale, part_refs, slope_ref, first_back_ref, second_back_ref, back_refs,
    value_ref, delta_ref, pencil, inner, returned,
):
    me = lax.axis_index("space")
    blocks = slope_ref.shape[0]
    block = first_back_ref.shape[1] // 2
    planes = part_refs[0].shape[0] // samples
    rows = part_refs[0].shape[1] // 2
    length_x = count * planes
    tile = 16 if rows % 16 == 0 else rows
    for step, part_ref in enumerate(part_refs):
        home = neighbour(me, -step, count)
        for sample in range(samples):
            for plane in range(planes):
                pencil[sample, home * planes + plane] = part_ref[sample * planes + plane]
    for at in range(blocks):
        lanes = slice(at * block, (at + 1) * block)
        for sample in range(samples):
            for start in range(0, rows, tile):
                pairs = [
                    (
                        pencil[sample, x, start : start + tile, lanes].astype(f32),
                        pencil[sample, x, rows + start : rows + start + tile, lanes].astype(f32),
                    )
                    for x in range(length_x)
                ]
                for x, (real, imag) in enumerate(short_transform(pairs, -1)):
                    base = (sample * length_x + x) * rows + start
                    value_ref[at, base : base + tile, :block] = (real * norm_scale).astype(bf16)
                    value_ref[at, base : base + tile, block:] = (imag * norm_scale).astype(bf16)
        back = jnp.dot(value_ref[at], second_back_ref[at], preferred_element_type=f32)
        delta = (back * slope_ref[at]).astype(bf16)
        delta_ref[at] = delta
        inner[at] = jnp.dot(delta, first_back_ref[at], preferred_element_type=f32)
        for sample in range(samples):
            for start in range(0, rows, tile):
                pairs = []
                for x in range(length_x):
                    base = (sample * length_x + x) * rows + start
                    pairs.append((inner[at, base : base + tile, :block], inner[at, base : base + tile, block:]))
                for x, (real, imag) in enumerate(short_transform(pairs, 1)):
                    returned[sample, x, start : start + tile, lanes] = real.astype(bf16)
                    returned[sample, x, rows + start : rows + start + tile, lanes] = imag.astype(bf16)
    for step, back_ref in enumerate(back_refs):
        home = neighbour(me, step, count)
        for sample in range(samples):
            for plane in range(planes):
                back_ref[sample * planes + plane] = returned[sample, home * planes + plane]


def weight_kernel(count, scale, exchange, groups, act_ref, flip_ref, value_ref, delta_ref, *term_refs):
    block = act_ref.shape[1] // 2
    for at in range(act_ref.shape[0]):
        lanes = slice(at * block, (at + 1) * block)
        for which, left, right in ((0, flip_ref, delta_ref), (1, act_ref, value_ref)):
            square = jnp.dot(left[at], right[at], preferred_element_type=f32) * scale
            real = square[:block, :block] + square[block:, block:]
            imag = square[:block, block:] - square[block:, :block]
            for part, term in ((0, real), (1, imag)):
                if exchange:
                    keep_ref, send_ref = term_refs[0], term_refs[-1]
                    piece = block // (2 * count)
                    split = term.reshape(count, 2, piece, block)
                    mine = lax.axis_index("dp") == 0
                    place = slice((2 * which + part) * piece, (2 * which + part + 1) * piece)
                    keep_ref[:, place, lanes] = jnp.where(mine, split[:, 0], split[:, 1])
                    send_ref[:, place, lanes] = jnp.where(mine, split[:, 1], split[:, 0]).astype(bf16)
                else:
                    term_refs[0][which, at, part] = term.astype(bf16)
    if exchange:
        me = lax.axis_index("space")
        for steps, out_ref in zip(groups, term_refs[1:-1]):
            for slot, step in enumerate(steps):
                out_ref[slot] = term_refs[-1][neighbour(me, step, count, True)]


def inverse_kernel(count, scale, table_ref, *refs):
    me = lax.axis_index("space")
    back_refs, out_ref = refs[:-1], refs[-1]
    for plane in range(out_ref.shape[0]):
        total = None
        for step, back_ref in enumerate(back_refs):
            table = table_ref[neighbour(me, -step, count)]
            product = jnp.dot(table, back_ref[plane], preferred_element_type=f32)
            total = product if total is None else total + product
        out_ref[plane] = (total * scale).astype(bf16)


def pair_sum_kernel(count, steps, keep_ref, got_ref, *refs):
    me = lax.axis_index("space")
    for slot, step in enumerate(steps):
        out_ref = refs[len(refs) - len(steps) + slot]
        out_ref[...] = (keep_ref[neighbour(me, step, count, True)] + got_ref[slot].astype(f32)).astype(out_ref.dtype)


def last_sum_kernel(*refs):
    got_refs, out_refs = refs[:-2], refs[-2:]
    blocks, _, piece, block = out_refs[0].shape
    total = got_refs[0][...]
    for got_ref in got_refs[1:]:
        total = total + got_ref[...].astype(f32)
    for at in range(blocks):
        for which in range(2):
            for part in range(2):
                place = (2 * which + part) * piece
                out_refs[which][at, part] = total[place : place + piece, at * block : (at + 1) * block]


def call(kernel, outs, args, scratch=(), loose=0, name=None):
    whole = pl.BlockSpec(memory_space=pltpu.VMEM)
    return pl.pallas_call(
        kernel,
        out_shape=tuple(outs),
        in_specs=[whole] * (len(args) - loose) + [pl.BlockSpec(memory_space=pl.ANY)] * loose,
        out_specs=(whole,) * len(outs),
        scratch_shapes=list(scratch),
        compiler_params=pltpu.CompilerParams(vmem_limit_bytes=vmem_bytes),
        name=name,
    )(*args)


def spread(values, count, folded=False):
    order = ring(count, folded)
    moved = []
    for step in range(1, count):
        pairs = [(order[at], order[(at + step) % count]) for at in range(count)]
        moved.append(lax.ppermute(values[step], "space", pairs))
    return [values[0]] + moved


def body(grad_out, saved_spectrum, w_first, bias_first, w_second):
    samples, planes, length_y, length_z, width = grad_out.shape
    blocks, _, block, _ = w_first.shape
    count = lax.axis_size("space")
    pair = lax.axis_size("dp")
    length_x = planes * count
    cells = length_y * length_z
    rows = cells // count
    lines = samples * length_x * rows
    slabs = samples * planes
    norm_scale = 1.0 / math.sqrt(length_x * cells)
    grad_scale = 1.0 / math.sqrt(length_x * cells * samples * pair)
    piece = block // (pair * count)
    exchange = pair == 2 and count > 1 and piece * pair * count == block and piece % 16 == 0
    inverse, factor = inverse_table(length_y, length_z, count)
    shape = jax.ShapeDtypeStruct
    slab = shape((slabs, 2 * rows, width), bf16)
    square = shape((blocks, 2 * block, 2 * block), bf16)
    tall = shape((blocks, lines, 2 * block), bf16)
    wide = shape((blocks, 2 * block, lines), bf16)

    parts = spread(
        call(
            functools.partial(forward_kernel, count, factor, length_y, length_z),
            [slab] * count,
            [grad_out.reshape(slabs, cells, width)],
            scratch=[pltpu.VMEM((count, 2 * rows, cells), bf16)],
            name="forward",
        ),
        count,
    )
    act, flip, slope, first_back, second_back = call(
        activation_kernel,
        [wide, wide, shape((blocks, lines, 2 * block), f32), square, square],
        [saved_spectrum.reshape(2, lines, width), w_first, bias_first, w_second],
        name="activation",
    )

    def filter_body(*refs):
        filter_kernel(
            count, samples, norm_scale, refs[:count], *refs[count : count + 3], refs[count + 3 : 2 * count + 3],
            *refs[2 * count + 3 :],
        )

    *backs, value, delta = call(
        filter_body,
        [slab] * count + [tall, tall],
        [*parts, slope, first_back, second_back],
        scratch=[
            pltpu.VMEM((samples, length_x, 2 * rows, width), bf16),
            pltpu.VMEM((blocks, lines, 2 * block), f32),
            pltpu.VMEM((samples, length_x, 2 * rows, width), bf16),
        ],
        name="filter",
    )
    backs = spread(backs, count)
    half = count // 2
    groups = (tuple(range(half, count)), tuple(range(half)))
    if exchange:
        terms = [shape((count, 4 * piece, width), f32)]
        terms += [shape((len(steps), 4 * piece, width), bf16) for steps in groups]
        scratch = [pltpu.VMEM((count, 4 * piece, width), bf16)]
    else:
        terms = [shape((2, blocks, 2, block, block), bf16)]
        scratch = []
    terms = call(
        functools.partial(weight_kernel, count, grad_scale, exchange, groups), terms, [act, flip, value, delta],
        scratch=scratch, name="weight",
    )
    if exchange:
        keep, *sends = terms
        got = [lax.ppermute(send, "dp", [(0, 1), (1, 0)]) for send in sends]
        sums = {}
        for at, steps in enumerate(groups):
            after = [backs[half]] if at == 1 else []
            outs = call(
                functools.partial(pair_sum_kernel, count, steps),
                [shape((4 * piece, width), bf16 if step else f32) for step in steps],
                [keep, got[at], *after],
                loose=len(after),
                name="pair_sum" + str(at),
            )
            sums.update(zip(steps, outs))
        grad_first, grad_second = call(
            last_sum_kernel, [shape((blocks, 2, piece, block), f32)] * 2, spread([sums[step] for step in range(count)], count, True), name="last_sum"
        )
    else:
        term = lax.psum_scatter(terms[0], "space", scatter_dimension=3, tiled=True)
        term = lax.psum_scatter(term, "dp", scatter_dimension=3, tiled=True).astype(f32)
        grad_first, grad_second = term[0], term[1]
    (grad_in,) = call(
        functools.partial(inverse_kernel, count, norm_scale / factor),
        [shape((slabs, cells, width), bf16)],
        [jnp.asarray(inverse), *backs],
        name="inverse",
    )
    return grad_in.reshape(grad_out.shape), grad_first, grad_second


def solution(mesh):
    in_specs = (
        P(("parts", "dp"), "space", None, None, "chan"),
        P(None, ("parts", "dp"), None, "space", None, "chan"),
        P("chan", None, None, None),
        P(None, "chan"),
        P("chan", None, None, None),
    )
    out_specs = (
        P(("parts", "dp"), "space", None, None, "chan"),
        P(("parts", "chan"), None, ("space", "dp"), None),
        P(("parts", "chan"), None, ("space", "dp"), None),
    )
    return jax.shard_map(body, mesh=mesh, in_specs=in_specs, out_specs=out_specs, check_vma=False)
```

```python
import functools
import math

import jax
import jax.numpy as jnp
import numpy as np
from jax import lax
from jax.experimental import pallas as pl
from jax.experimental.pallas import tpu as pltpu
from jax.sharding import PartitionSpec as P

inv_root_two = 1.0 / math.sqrt(2.0)
inv_root_tau = 1.0 / math.sqrt(2.0 * math.pi)
f32 = jnp.float32
bf16 = jnp.bfloat16
vmem_bytes = 24 * 1024 * 1024


def phase_table(length_y, length_z):
    whole = math.lcm(length_y, length_z)
    y = np.arange(length_y)
    z = np.arange(length_z)
    turns = (
        (y[:, None, None, None] * y[None, None, :, None]) * (whole // length_y)
        + (z[None, :, None, None] * z[None, None, None, :]) * (whole // length_z)
    ) % whole
    cells = length_y * length_z
    return turns.reshape(cells, cells) * (2.0 * math.pi / whole)


def round_scaled(table):
    levels = np.unique(np.abs(table).round(12))
    factors = np.linspace(1.0, 2.0, 2049)[:-1]
    scaled = factors[:, None] * levels
    error = np.abs(scaled.astype(bf16).astype(np.float64) / factors[:, None] - levels).max(axis=1)
    factor = float(factors[np.argmin(error)])
    return (table * factor).astype(bf16), factor


def inverse_table(length_y, length_z, count):
    angles = phase_table(length_y, length_z)
    cells = length_y * length_z
    rows = cells // count
    both = np.stack([np.cos(angles), -np.sin(angles)]).reshape(2, count, rows, cells)
    table, factor = round_scaled(both.transpose(1, 3, 0, 2).reshape(count, cells, 2 * rows))
    return table, factor


def turn(real, imag, step, length, orient):
    step %= length
    if step == 0:
        return real, imag
    if 2 * step == length:
        return -real, -imag
    if 4 * step == length or 4 * step == 3 * length:
        sign = orient if 4 * step == length else -orient
        return (-imag, real) if sign > 0 else (imag, -real)
    cosine = math.cos(2.0 * math.pi * step / length)
    sine = orient * math.sin(2.0 * math.pi * step / length)
    return cosine * real - sine * imag, sine * real + cosine * imag


def short_transform(pairs, orient):
    length = len(pairs)
    if length == 1:
        return pairs
    if length % 2 == 0:
        even = short_transform(pairs[0::2], orient)
        odd = short_transform(pairs[1::2], orient)
        half = length // 2
        out = [None] * length
        for k in range(half):
            real, imag = turn(*odd[k], k, length, orient)
            out[k] = (even[k][0] + real, even[k][1] + imag)
            out[k + half] = (even[k][0] - real, even[k][1] - imag)
        return out
    out = []
    for k in range(length):
        terms = [turn(*pairs[x], k * x, length, orient) for x in range(length)]
        out.append((sum(t[0] for t in terms), sum(t[1] for t in terms)))
    return out


def paired(weight_ref, at):
    real = weight_ref[at, 0]
    imag = weight_ref[at, 1]
    return jnp.concatenate(
        [jnp.concatenate([real, imag], axis=1), jnp.concatenate([-imag, real], axis=1)], axis=0
    )


def wave_rows(length, cells, inner, outer):
    row = lax.broadcasted_iota(jnp.int32, (length, cells), 0)
    cell = lax.broadcasted_iota(jnp.int32, (length, cells), 1)
    turns = lax.rem(row * lax.rem(cell // inner, outer), length)
    turns = jnp.where(2 * turns > length, turns - length, turns)
    half = turns.astype(f32) * (math.pi / length)
    square = half * half
    sine, cosine = jnp.zeros_like(half), jnp.zeros_like(half)
    for power in range(7, -1, -1):
        sign = -1.0 if power % 2 else 1.0
        cosine = cosine * square + sign / math.factorial(2 * power)
        sine = sine * square + sign / math.factorial(2 * power + 1)
    sine = sine * half
    return 1.0 - 2.0 * sine * sine, 2.0 * sine * cosine


def ring(count, folded):
    if not folded:
        return list(range(count))
    return [0] + list(range(1, count, 2)) + list(range(count - 2 + count % 2, 0, -2))


def neighbour(me, step, count, folded=False):
    order = ring(count, folded)
    if not folded:
        return lax.rem(me + step + count, count)
    home = jnp.int32(0)
    for at, here in enumerate(order):
        home = jnp.where(me == here, order[(at + step) % count], home)
    return home


def forward_kernel(count, factor, length_y, length_z, cell_ref, *refs):
    out_refs, table_ref = refs[:-1], refs[-1]
    me = lax.axis_index("space")
    planes, cells, _ = cell_ref.shape
    rows = cells // count
    cos_y, sin_y = wave_rows(length_y, cells, length_z, length_y)
    cos_z, sin_z = wave_rows(length_z, cells, 1, length_z)
    cos_z, sin_z = cos_z * factor, sin_z * factor
    each = length_y // count
    for ky in range(length_y):
        cos_k, sin_k = cos_y[ky : ky + 1], sin_y[ky : ky + 1]
        start = ky % each * length_z
        table_ref[ky // each, start : start + length_z] = (cos_z * cos_k - sin_z * sin_k).astype(bf16)
        table_ref[ky // each, rows + start : rows + start + length_z] = (
            -(cos_z * sin_k) - sin_z * cos_k
        ).astype(bf16)
    for step, out_ref in enumerate(out_refs):
        table = table_ref[neighbour(me, step, count)]
        for plane in range(planes):
            product = jnp.dot(table, cell_ref[plane], preferred_element_type=f32) * (1.0 / factor)
            out_ref[plane] = product.astype(bf16)


def activation_kernel(
    saved_ref, first_ref, bias_ref, second_ref, act_ref, flip_ref, slope_ref, first_back_ref, second_back_ref
):
    count, _, block, _ = first_ref.shape
    for at in range(count):
        lanes = slice(at * block, (at + 1) * block)
        first = paired(first_ref, at)
        first_back_ref[at] = first.T
        second_back_ref[at] = paired(second_ref, at).T
        saved = jnp.concatenate([saved_ref[0, :, lanes], saved_ref[1, :, lanes]], axis=1)
        bias = jnp.concatenate([bias_ref[0:1, lanes], bias_ref[1:2, lanes]], axis=1).astype(f32)
        pre = jnp.dot(saved, first, preferred_element_type=f32) + bias
        share = 0.5 * (1.0 + lax.erf(pre * inv_root_two))
        act_ref[at] = (pre * share).astype(bf16).T
        flip_ref[at] = saved.T
        slope_ref[at] = share + pre * jnp.exp(-0.5 * pre * pre) * inv_root_tau


def filter_kernel(
    count, samples, norm_scale, part_refs, slope_ref, first_back_ref, second_back_ref, back_refs,
    value_ref, delta_ref, pencil, inner, returned,
):
    me = lax.axis_index("space")
    blocks = slope_ref.shape[0]
    block = first_back_ref.shape[1] // 2
    planes = part_refs[0].shape[0] // samples
    rows = part_refs[0].shape[1] // 2
    length_x = count * planes
    tile = 16 if rows % 16 == 0 else rows
    for step, part_ref in enumerate(part_refs):
        home = neighbour(me, -step, count)
        for sample in range(samples):
            for plane in range(planes):
                pencil[sample, home * planes + plane] = part_ref[sample * planes + plane]
    for at in range(blocks):
        lanes = slice(at * block, (at + 1) * block)
        for sample in range(samples):
            for start in range(0, rows, tile):
                pairs = [
                    (
                        pencil[sample, x, start : start + tile, lanes].astype(f32),
                        pencil[sample, x, rows + start : rows + start + tile, lanes].astype(f32),
                    )
                    for x in range(length_x)
                ]
                for x, (real, imag) in enumerate(short_transform(pairs, -1)):
                    base = (sample * length_x + x) * rows + start
                    value_ref[at, base : base + tile, :block] = (real * norm_scale).astype(bf16)
                    value_ref[at, base : base + tile, block:] = (imag * norm_scale).astype(bf16)
        back = jnp.dot(value_ref[at], second_back_ref[at], preferred_element_type=f32)
        delta = (back * slope_ref[at]).astype(bf16)
        delta_ref[at] = delta
        inner[at] = jnp.dot(delta, first_back_ref[at], preferred_element_type=f32)
        for sample in range(samples):
            for start in range(0, rows, tile):
                pairs = []
                for x in range(length_x):
                    base = (sample * length_x + x) * rows + start
                    pairs.append((inner[at, base : base + tile, :block], inner[at, base : base + tile, block:]))
                for x, (real, imag) in enumerate(short_transform(pairs, 1)):
                    returned[sample, x, start : start + tile, lanes] = real.astype(bf16)
                    returned[sample, x, rows + start : rows + start + tile, lanes] = imag.astype(bf16)
    for step, back_ref in enumerate(back_refs):
        home = neighbour(me, step, count)
        for sample in range(samples):
            for plane in range(planes):
                back_ref[sample * planes + plane] = returned[sample, home * planes + plane]


def weight_kernel(count, scale, exchange, groups, act_ref, flip_ref, value_ref, delta_ref, *term_refs):
    block = act_ref.shape[1] // 2
    for at in range(act_ref.shape[0]):
        lanes = slice(at * block, (at + 1) * block)
        for which, left, right in ((0, flip_ref, delta_ref), (1, act_ref, value_ref)):
            square = jnp.dot(left[at], right[at], preferred_element_type=f32) * scale
            real = square[:block, :block] + square[block:, block:]
            imag = square[:block, block:] - square[block:, :block]
            for part, term in ((0, real), (1, imag)):
                if exchange:
                    keep_ref, send_ref = term_refs[0], term_refs[-1]
                    piece = block // (2 * count)
                    split = term.reshape(count, 2, piece, block)
                    mine = lax.axis_index("dp") == 0
                    place = slice((2 * which + part) * piece, (2 * which + part + 1) * piece)
                    keep_ref[:, place, lanes] = jnp.where(mine, split[:, 0], split[:, 1])
                    send_ref[:, place, lanes] = jnp.where(mine, split[:, 1], split[:, 0]).astype(bf16)
                else:
                    term_refs[0][which, at, part] = term.astype(bf16)
    if exchange:
        me = lax.axis_index("space")
        for steps, out_ref in zip(groups, term_refs[1:-1]):
            for slot, step in enumerate(steps):
                out_ref[slot] = term_refs[-1][neighbour(me, step, count, True)]


def inverse_kernel(count, scale, table_ref, *refs):
    me = lax.axis_index("space")
    back_refs, out_ref = refs[:-1], refs[-1]
    for plane in range(out_ref.shape[0]):
        total = None
        for step, back_ref in enumerate(back_refs):
            table = table_ref[neighbour(me, -step, count)]
            product = jnp.dot(table, back_ref[plane], preferred_element_type=f32)
            total = product if total is None else total + product
        out_ref[plane] = (total * scale).astype(bf16)


def pair_sum_kernel(count, steps, keep_ref, got_ref, *refs):
    me = lax.axis_index("space")
    for slot, step in enumerate(steps):
        out_ref = refs[len(refs) - len(steps) + slot]
        out_ref[...] = (keep_ref[neighbour(me, step, count, True)] + got_ref[slot].astype(f32)).astype(out_ref.dtype)


def last_sum_kernel(*refs):
    got_refs, out_refs = refs[:-2], refs[-2:]
    blocks, _, piece, block = out_refs[0].shape
    total = got_refs[0][...]
    for got_ref in got_refs[1:]:
        total = total + got_ref[...].astype(f32)
    for at in range(blocks):
        for which in range(2):
            for part in range(2):
                place = (2 * which + part) * piece
                out_refs[which][at, part] = total[place : place + piece, at * block : (at + 1) * block]


def call(kernel, outs, args, scratch=(), loose=0, name=None):
    whole = pl.BlockSpec(memory_space=pltpu.VMEM)
    return pl.pallas_call(
        kernel,
        out_shape=tuple(outs),
        in_specs=[whole] * (len(args) - loose) + [pl.BlockSpec(memory_space=pl.ANY)] * loose,
        out_specs=(whole,) * len(outs),
        scratch_shapes=list(scratch),
        compiler_params=pltpu.CompilerParams(vmem_limit_bytes=vmem_bytes),
        name=name,
    )(*args)


def spread(values, count, folded=False):
    order = ring(count, folded)
    moved = []
    for step in range(1, count):
        pairs = [(order[at], order[(at + step) % count]) for at in range(count)]
        moved.append(lax.ppermute(values[step], "space", pairs))
    return [values[0]] + moved


def body(grad_out, saved_spectrum, w_first, bias_first, w_second):
    samples, planes, length_y, length_z, width = grad_out.shape
    blocks, _, block, _ = w_first.shape
    count = lax.axis_size("space")
    pair = lax.axis_size("dp")
    length_x = planes * count
    cells = length_y * length_z
    rows = cells // count
    lines = samples * length_x * rows
    slabs = samples * planes
    norm_scale = 1.0 / math.sqrt(length_x * cells)
    grad_scale = 1.0 / math.sqrt(length_x * cells * samples * pair)
    piece = block // (pair * count)
    exchange = pair == 2 and count > 1 and piece * pair * count == block and piece % 16 == 0
    inverse, factor = inverse_table(length_y, length_z, count)
    shape = jax.ShapeDtypeStruct
    slab = shape((slabs, 2 * rows, width), bf16)
    square = shape((blocks, 2 * block, 2 * block), bf16)
    tall = shape((blocks, lines, 2 * block), bf16)
    wide = shape((blocks, 2 * block, lines), bf16)

    parts = spread(
        call(
            functools.partial(forward_kernel, count, factor, length_y, length_z),
            [slab] * count,
            [grad_out.reshape(slabs, cells, width)],
            scratch=[pltpu.VMEM((count, 2 * rows, cells), bf16)],
            name="forward",
        ),
        count,
    )
    act, flip, slope, first_back, second_back = call(
        activation_kernel,
        [wide, wide, shape((blocks, lines, 2 * block), f32), square, square],
        [saved_spectrum.reshape(2, lines, width), w_first, bias_first, w_second],
        name="activation",
    )

    def filter_body(*refs):
        filter_kernel(
            count, samples, norm_scale, refs[:count], *refs[count : count + 3], refs[count + 3 : 2 * count + 3],
            *refs[2 * count + 3 :],
        )

    *backs, value, delta = call(
        filter_body,
        [slab] * count + [tall, tall],
        [*parts, slope, first_back, second_back],
        scratch=[
            pltpu.VMEM((samples, length_x, 2 * rows, width), bf16),
            pltpu.VMEM((blocks, lines, 2 * block), f32),
            pltpu.VMEM((samples, length_x, 2 * rows, width), bf16),
        ],
        name="filter",
    )
    backs = spread(backs, count)
    half = count // 2
    groups = (tuple(range(half, count)), tuple(range(half)))
    if exchange:
        terms = [shape((count, 4 * piece, width), f32)]
        terms += [shape((len(steps), 4 * piece, width), bf16) for steps in groups]
        scratch = [pltpu.VMEM((count, 4 * piece, width), bf16)]
    else:
        terms = [shape((2, blocks, 2, block, block), bf16)]
        scratch = []
    terms = call(
        functools.partial(weight_kernel, count, grad_scale, exchange, groups), terms, [act, flip, value, delta],
        scratch=scratch, name="weight",
    )
    if exchange:
        keep, *sends = terms
        got = [lax.ppermute(send, "dp", [(0, 1), (1, 0)]) for send in sends]
        sums = {}
        for at, steps in enumerate(groups):
            after = [backs[half]] if at == 1 else []
            outs = call(
                functools.partial(pair_sum_kernel, count, steps),
                [shape((4 * piece, width), bf16 if step else f32) for step in steps],
                [keep, got[at], *after],
                loose=len(after),
                name="pair_sum" + str(at),
            )
            sums.update(zip(steps, outs))
        grad_first, grad_second = call(
            last_sum_kernel, [shape((blocks, 2, piece, block), f32)] * 2, spread([sums[step] for step in range(count)], count, True), name="last_sum"
        )
    else:
        term = lax.psum_scatter(terms[0], "space", scatter_dimension=3, tiled=True)
        term = lax.psum_scatter(term, "dp", scatter_dimension=3, tiled=True).astype(f32)
        grad_first, grad_second = term[0], term[1]
    (grad_in,) = call(
        functools.partial(inverse_kernel, count, norm_scale / factor),
        [shape((slabs, cells, width), bf16)],
        [jnp.asarray(inverse), *backs],
        name="inverse",
    )
    return grad_in.reshape(grad_out.shape), grad_first, grad_second


def solution(mesh):
    in_specs = (
        P(("parts", "dp"), "space", None, None, "chan"),
        P(None, ("parts", "dp"), None, "space", None, "chan"),
        P("chan", None, None, None),
        P(None, "chan"),
        P("chan", None, None, None),
    )
    out_specs = (
        P(("parts", "dp"), "space", None, None, "chan"),
        P(("parts", "chan"), None, ("space", "dp"), None),
        P(("parts", "chan"), None, ("space", "dp"), None),
    )
    return jax.shard_map(body, mesh=mesh, in_specs=in_specs, out_specs=out_specs, check_vma=False)
```

```python
import functools
import math

import jax
import jax.numpy as jnp
import numpy as np
from jax import lax
from jax.experimental import pallas as pl
from jax.experimental.pallas import tpu as pltpu
from jax.sharding import PartitionSpec as P

inv_root_two = 1.0 / math.sqrt(2.0)
inv_root_tau = 1.0 / math.sqrt(2.0 * math.pi)
f32 = jnp.float32
bf16 = jnp.bfloat16
vmem_bytes = 24 * 1024 * 1024


def phase_table(length_y, length_z):
    whole = math.lcm(length_y, length_z)
    y = np.arange(length_y)
    z = np.arange(length_z)
    turns = (
        (y[:, None, None, None] * y[None, None, :, None]) * (whole // length_y)
        + (z[None, :, None, None] * z[None, None, None, :]) * (whole // length_z)
    ) % whole
    cells = length_y * length_z
    return turns.reshape(cells, cells) * (2.0 * math.pi / whole)


def round_scaled(table):
    levels = np.unique(np.abs(table).round(12))
    factors = np.linspace(1.0, 2.0, 2049)[:-1]
    scaled = factors[:, None] * levels
    error = np.abs(scaled.astype(bf16).astype(np.float64) / factors[:, None] - levels).max(axis=1)
    factor = float(factors[np.argmin(error)])
    return (table * factor).astype(bf16), factor


def inverse_table(length_y, length_z, count):
    angles = phase_table(length_y, length_z)
    cells = length_y * length_z
    rows = cells // count
    both = np.stack([np.cos(angles), -np.sin(angles)]).reshape(2, count, rows, cells)
    table, factor = round_scaled(both.transpose(1, 3, 0, 2).reshape(count, cells, 2 * rows))
    return table, factor


def turn(real, imag, step, length, orient):
    step %= length
    if step == 0:
        return real, imag
    if 2 * step == length:
        return -real, -imag
    if 4 * step == length or 4 * step == 3 * length:
        sign = orient if 4 * step == length else -orient
        return (-imag, real) if sign > 0 else (imag, -real)
    cosine = math.cos(2.0 * math.pi * step / length)
    sine = orient * math.sin(2.0 * math.pi * step / length)
    return cosine * real - sine * imag, sine * real + cosine * imag


def short_transform(pairs, orient):
    length = len(pairs)
    if length == 1:
        return pairs
    if length % 2 == 0:
        even = short_transform(pairs[0::2], orient)
        odd = short_transform(pairs[1::2], orient)
        half = length // 2
        out = [None] * length
        for k in range(half):
            real, imag = turn(*odd[k], k, length, orient)
            out[k] = (even[k][0] + real, even[k][1] + imag)
            out[k + half] = (even[k][0] - real, even[k][1] - imag)
        return out
    out = []
    for k in range(length):
        terms = [turn(*pairs[x], k * x, length, orient) for x in range(length)]
        out.append((sum(t[0] for t in terms), sum(t[1] for t in terms)))
    return out


def paired(weight_ref, at):
    real = weight_ref[at, 0]
    imag = weight_ref[at, 1]
    return jnp.concatenate(
        [jnp.concatenate([real, imag], axis=1), jnp.concatenate([-imag, real], axis=1)], axis=0
    )


def wave_rows(length, cells, inner, outer):
    row = lax.broadcasted_iota(jnp.int32, (length, cells), 0)
    cell = lax.broadcasted_iota(jnp.int32, (length, cells), 1)
    turns = lax.rem(row * lax.rem(cell // inner, outer), length)
    turns = jnp.where(2 * turns > length, turns - length, turns)
    half = turns.astype(f32) * (math.pi / length)
    square = half * half
    sine, cosine = jnp.zeros_like(half), jnp.zeros_like(half)
    for power in range(7, -1, -1):
        sign = -1.0 if power % 2 else 1.0
        cosine = cosine * square + sign / math.factorial(2 * power)
        sine = sine * square + sign / math.factorial(2 * power + 1)
    sine = sine * half
    return 1.0 - 2.0 * sine * sine, 2.0 * sine * cosine


def ring(count, folded):
    if not folded:
        return list(range(count))
    return [0] + list(range(1, count, 2)) + list(range(count - 2 + count % 2, 0, -2))


def neighbour(me, step, count, folded=False):
    order = ring(count, folded)
    if not folded:
        return lax.rem(me + step + count, count)
    home = jnp.int32(0)
    for at, here in enumerate(order):
        home = jnp.where(me == here, order[(at + step) % count], home)
    return home


def forward_kernel(count, factor, scale, length_y, length_z, cell_ref, *refs):
    out_refs, table_ref = refs[:-1], refs[-1]
    me = lax.axis_index("space")
    planes, cells, _ = cell_ref.shape
    rows = cells // count
    cos_y, sin_y = wave_rows(length_y, cells, length_z, length_y)
    cos_z, sin_z = wave_rows(length_z, cells, 1, length_z)
    cos_z, sin_z = cos_z * factor, sin_z * factor
    each = length_y // count
    for ky in range(length_y):
        cos_k, sin_k = cos_y[ky : ky + 1], sin_y[ky : ky + 1]
        start = ky % each * length_z
        table_ref[ky // each, start : start + length_z] = (cos_z * cos_k - sin_z * sin_k).astype(bf16)
        table_ref[ky // each, rows + start : rows + start + length_z] = (
            -(cos_z * sin_k) - sin_z * cos_k
        ).astype(bf16)
    for step, out_ref in enumerate(out_refs):
        table = table_ref[neighbour(me, step, count)]
        for plane in range(planes):
            product = jnp.dot(table, cell_ref[plane], preferred_element_type=f32) * scale
            out_ref[plane] = product.astype(bf16)


def activation_kernel(
    saved_ref, first_ref, bias_ref, second_ref, act_ref, flip_ref, slope_ref, first_back_ref, second_back_ref
):
    count, _, block, _ = first_ref.shape
    for at in range(count):
        lanes = slice(at * block, (at + 1) * block)
        first = paired(first_ref, at)
        first_back_ref[at] = first.T
        second_back_ref[at] = paired(second_ref, at).T
        saved = jnp.concatenate([saved_ref[0, :, lanes], saved_ref[1, :, lanes]], axis=1)
        bias = jnp.concatenate([bias_ref[0:1, lanes], bias_ref[1:2, lanes]], axis=1).astype(f32)
        pre = jnp.dot(saved, first, preferred_element_type=f32) + bias
        share = 0.5 * (1.0 + lax.erf(pre * inv_root_two))
        act_ref[at] = (pre * share).astype(bf16).T
        flip_ref[at] = saved.T
        slope_ref[at] = share + pre * jnp.exp(-0.5 * pre * pre) * inv_root_tau


def filter_kernel(
    count, samples, part_refs, slope_ref, first_back_ref, second_back_ref, back_refs,
    value_ref, delta_ref, pencil, inner, returned,
):
    me = lax.axis_index("space")
    blocks = slope_ref.shape[0]
    block = first_back_ref.shape[1] // 2
    planes = part_refs[0].shape[0] // samples
    rows = part_refs[0].shape[1] // 2
    length_x = count * planes
    tile = 16 if rows % 16 == 0 else rows
    for step, part_ref in enumerate(part_refs):
        home = neighbour(me, -step, count)
        for sample in range(samples):
            for plane in range(planes):
                pencil[sample, home * planes + plane] = part_ref[sample * planes + plane]
    for at in range(blocks):
        lanes = slice(at * block, (at + 1) * block)
        for sample in range(samples):
            for start in range(0, rows, tile):
                pairs = [
                    (
                        pencil[sample, x, start : start + tile, lanes].astype(f32),
                        pencil[sample, x, rows + start : rows + start + tile, lanes].astype(f32),
                    )
                    for x in range(length_x)
                ]
                for x, (real, imag) in enumerate(short_transform(pairs, -1)):
                    base = (sample * length_x + x) * rows + start
                    value_ref[at, base : base + tile, :block] = real.astype(bf16)
                    value_ref[at, base : base + tile, block:] = imag.astype(bf16)
        back = jnp.dot(value_ref[at], second_back_ref[at], preferred_element_type=f32)
        delta = (back * slope_ref[at]).astype(bf16)
        delta_ref[at] = delta
        inner[at] = jnp.dot(delta, first_back_ref[at], preferred_element_type=f32)
        for sample in range(samples):
            for start in range(0, rows, tile):
                pairs = []
                for x in range(length_x):
                    base = (sample * length_x + x) * rows + start
                    pairs.append((inner[at, base : base + tile, :block], inner[at, base : base + tile, block:]))
                for x, (real, imag) in enumerate(short_transform(pairs, 1)):
                    returned[sample, x, start : start + tile, lanes] = real.astype(bf16)
                    returned[sample, x, rows + start : rows + start + tile, lanes] = imag.astype(bf16)
    for step, back_ref in enumerate(back_refs):
        home = neighbour(me, step, count)
        for sample in range(samples):
            for plane in range(planes):
                back_ref[sample * planes + plane] = returned[sample, home * planes + plane]


def weight_kernel(count, scale, exchange, groups, act_ref, flip_ref, value_ref, delta_ref, *term_refs):
    block = act_ref.shape[1] // 2
    for at in range(act_ref.shape[0]):
        lanes = slice(at * block, (at + 1) * block)
        for which, left, right in ((0, flip_ref, delta_ref), (1, act_ref, value_ref)):
            square = jnp.dot(left[at], right[at], preferred_element_type=f32)
            real = (square[:block, :block] + square[block:, block:]) * scale
            imag = (square[:block, block:] - square[block:, :block]) * scale
            for part, term in ((0, real), (1, imag)):
                if exchange:
                    keep_ref, send_ref = term_refs[0], term_refs[-1]
                    piece = block // (2 * count)
                    split = term.reshape(count, 2, piece, block)
                    mine = lax.axis_index("dp") == 0
                    place = slice((2 * which + part) * piece, (2 * which + part + 1) * piece)
                    keep_ref[:, place, lanes] = jnp.where(mine, split[:, 0], split[:, 1])
                    send_ref[:, place, lanes] = jnp.where(mine, split[:, 1], split[:, 0]).astype(bf16)
                else:
                    term_refs[0][which, at, part] = term.astype(bf16)
    if exchange:
        me = lax.axis_index("space")
        for steps, out_ref in zip(groups, term_refs[1:-1]):
            for slot, step in enumerate(steps):
                out_ref[slot] = term_refs[-1][neighbour(me, step, count, True)]


def inverse_kernel(count, scale, table_ref, *refs):
    me = lax.axis_index("space")
    back_refs, out_ref = refs[:-1], refs[-1]
    for plane in range(out_ref.shape[0]):
        total = None
        for step, back_ref in enumerate(back_refs):
            table = table_ref[neighbour(me, -step, count)]
            product = jnp.dot(table, back_ref[plane], preferred_element_type=f32)
            total = product if total is None else total + product
        out_ref[plane] = (total * scale).astype(bf16)


def pair_sum_kernel(count, steps, keep_ref, got_ref, *refs):
    me = lax.axis_index("space")
    for slot, step in enumerate(steps):
        out_ref = refs[len(refs) - len(steps) + slot]
        out_ref[...] = (keep_ref[neighbour(me, step, count, True)] + got_ref[slot].astype(f32)).astype(out_ref.dtype)


def last_sum_kernel(*refs):
    got_refs, out_refs = refs[:-2], refs[-2:]
    blocks, _, piece, block = out_refs[0].shape
    total = got_refs[0][...]
    for got_ref in got_refs[1:]:
        total = total + got_ref[...].astype(f32)
    for at in range(blocks):
        for which in range(2):
            for part in range(2):
                place = (2 * which + part) * piece
                out_refs[which][at, part] = total[place : place + piece, at * block : (at + 1) * block]


def call(kernel, outs, args, scratch=(), loose=0, name=None):
    whole = pl.BlockSpec(memory_space=pltpu.VMEM)
    return pl.pallas_call(
        kernel,
        out_shape=tuple(outs),
        in_specs=[whole] * (len(args) - loose) + [pl.BlockSpec(memory_space=pl.ANY)] * loose,
        out_specs=(whole,) * len(outs),
        scratch_shapes=list(scratch),
        compiler_params=pltpu.CompilerParams(vmem_limit_bytes=vmem_bytes),
        name=name,
    )(*args)


def spread(values, count, folded=False):
    order = ring(count, folded)
    moved = []
    for step in range(1, count):
        pairs = [(order[at], order[(at + step) % count]) for at in range(count)]
        moved.append(lax.ppermute(values[step], "space", pairs))
    return [values[0]] + moved


def body(grad_out, saved_spectrum, w_first, bias_first, w_second):
    samples, planes, length_y, length_z, width = grad_out.shape
    blocks, _, block, _ = w_first.shape
    count = lax.axis_size("space")
    pair = lax.axis_size("dp")
    length_x = planes * count
    cells = length_y * length_z
    rows = cells // count
    lines = samples * length_x * rows
    slabs = samples * planes
    norm_scale = 1.0 / math.sqrt(length_x * cells)
    grad_scale = 1.0 / math.sqrt(length_x * cells * samples * pair)
    piece = block // (pair * count)
    exchange = pair == 2 and count > 1 and piece * pair * count == block and piece % 16 == 0
    inverse, factor = inverse_table(length_y, length_z, count)
    shape = jax.ShapeDtypeStruct
    slab = shape((slabs, 2 * rows, width), bf16)
    square = shape((blocks, 2 * block, 2 * block), bf16)
    tall = shape((blocks, lines, 2 * block), bf16)
    wide = shape((blocks, 2 * block, lines), bf16)

    parts = spread(
        call(
            functools.partial(forward_kernel, count, factor, norm_scale / factor, length_y, length_z),
            [slab] * count,
            [grad_out.reshape(slabs, cells, width)],
            scratch=[pltpu.VMEM((count, 2 * rows, cells), bf16)],
            name="forward",
        ),
        count,
    )
    act, flip, slope, first_back, second_back = call(
        activation_kernel,
        [wide, wide, shape((blocks, lines, 2 * block), f32), square, square],
        [saved_spectrum.reshape(2, lines, width), w_first, bias_first, w_second],
        name="activation",
    )

    def filter_body(*refs):
        filter_kernel(
            count, samples, refs[:count], *refs[count : count + 3], refs[count + 3 : 2 * count + 3],
            *refs[2 * count + 3 :],
        )

    *backs, value, delta = call(
        filter_body,
        [slab] * count + [tall, tall],
        [*parts, slope, first_back, second_back],
        scratch=[
            pltpu.VMEM((samples, length_x, 2 * rows, width), bf16),
            pltpu.VMEM((blocks, lines, 2 * block), f32),
            pltpu.VMEM((samples, length_x, 2 * rows, width), bf16),
        ],
        name="filter",
    )
    backs = spread(backs, count)
    half = count // 2
    groups = (tuple(range(half, count)), tuple(range(half)))
    if exchange:
        terms = [shape((count, 4 * piece, width), f32)]
        terms += [shape((len(steps), 4 * piece, width), bf16) for steps in groups]
        scratch = [pltpu.VMEM((count, 4 * piece, width), bf16)]
    else:
        terms = [shape((2, blocks, 2, block, block), bf16)]
        scratch = []
    terms = call(
        functools.partial(weight_kernel, count, grad_scale, exchange, groups), terms, [act, flip, value, delta],
        scratch=scratch, name="weight",
    )
    if exchange:
        keep, *sends = terms
        got = [lax.ppermute(send, "dp", [(0, 1), (1, 0)]) for send in sends]
        sums = {}
        for at, steps in enumerate(groups):
            after = [backs[half]] if at == 1 else []
            outs = call(
                functools.partial(pair_sum_kernel, count, steps),
                [shape((4 * piece, width), bf16 if step else f32) for step in steps],
                [keep, got[at], *after],
                loose=len(after),
                name="pair_sum" + str(at),
            )
            sums.update(zip(steps, outs))
        grad_first, grad_second = call(
            last_sum_kernel, [shape((blocks, 2, piece, block), f32)] * 2, spread([sums[step] for step in range(count)], count, True), name="last_sum"
        )
    else:
        term = lax.psum_scatter(terms[0], "space", scatter_dimension=3, tiled=True)
        term = lax.psum_scatter(term, "dp", scatter_dimension=3, tiled=True).astype(f32)
        grad_first, grad_second = term[0], term[1]
    (grad_in,) = call(
        functools.partial(inverse_kernel, count, norm_scale / factor),
        [shape((slabs, cells, width), bf16)],
        [jnp.asarray(inverse), *backs],
        name="inverse",
    )
    return grad_in.reshape(grad_out.shape), grad_first, grad_second


def solution(mesh):
    in_specs = (
        P(("parts", "dp"), "space", None, None, "chan"),
        P(None, ("parts", "dp"), None, "space", None, "chan"),
        P("chan", None, None, None),
        P(None, "chan"),
        P("chan", None, None, None),
    )
    out_specs = (
        P(("parts", "dp"), "space", None, None, "chan"),
        P(("parts", "chan"), None, ("space", "dp"), None),
        P(("parts", "chan"), None, ("space", "dp"), None),
    )
    return jax.shard_map(body, mesh=mesh, in_specs=in_specs, out_specs=out_specs, check_vma=False)
```
